512 devices in a mesh: gx: 8 (over y_lo, core), gy: 8 (over y_hi, x), gz: 8 (over z).
Axes of the slice: x: 4, y: 8 (y_hi: 2, y_lo: 4; y = y_hi * 4 + y_lo), z: 8, core: 2. Of those that a mesh axis runs over, the one named last changes fastest.
Arguments:
- positions: float32 [512, 3, 72], P(('gx', 'gy', 'gz')), may hold values from 0.6 to 11.4, as said below
- species: int32 [512, 72], P(('gx', 'gy', 'gz')), may hold values from 0 to 3
- site_atom: int32 [512, 72], P(('gx', 'gy', 'gz')), may hold values from 0 to 71, as said below
- edge_center: int32 [512, 1152], P(('gx', 'gy', 'gz')), may hold values from 0 to 71, as said below
- edge_other: int32 [512, 1152], P(('gx', 'gy', 'gz')), may hold values from 0 to 255, as said below
- edge_count: int32 [512], P(('gx', 'gy', 'gz')), may hold values from 240 to 1152, as said below
- w_in: float32 [128, 16], replicated, may hold values from -1.5 to 1.5
- w_two: float32 [64, 128], replicated, may hold values from -0.5 to 0.5
- w_env: float32 [64, 64], replicated, may hold values from -0.75 to 0.75
- w_value: float32 [64, 64], replicated, may hold values from -0.75 to 0.75
- w_latent: float32 [128, 256], replicated, may hold values from -0.375 to 0.375
- w_out: float32 [64, 128], replicated, may hold values from -0.5 to 0.5
- readout: float32 [64], replicated, may hold values from -0.75 to 0.75
Outputs:
- forces: float32 [512, 3, 72], P(('gx', 'gy', 'gz'))
- site_energy: float32 [512, 72], P(('gx', 'gy', 'gz'))
- virial: float32 [3, 3], replicated
The draws below stay inside these ranges and needn't reach their ends.
Inputs may be any that keep to these rules, and one draw needn't show every extreme that they name: `positions`: the atom at lattice site (i, j, k) has coordinates within 0.4 of (2 i + 1, 2 j + 1, 2 k + 1). `site_atom`: each domain's row is a permutation of its atoms. `edge_center`: each atom is the center of exactly 16 slots of its domain. `edge_other`: the cell of the extended grid one of the 26 nonzero steps away from the center's own cell (its site (i, j, k) sits at cell (i + 1, j + 1, k + 1)); the 16 slots of one center take distinct steps. `edge_count`: edge slots at or after a domain's count are padding.
All inputs are finite; a program needn't handle non-finite values.
Results may differ from the reference program's by a relative error of at most 0.0003.
Values sent between devices are 32-bit elements; how exact they have to be, the bound alone decides.
No kernel may reach another device: no remote copies, remote signals or barrier semaphores. Data moves between devices by JAX's collectives and lax.ppermute only.
A program may use at most 64 MiB of HBM per device.

```python
import math
import jax
import jax.numpy as jnp
from jax import lax

CELLS = 6
LAYERS = 2
NEIGH = 16
ATOMS_DEV = 72
EDGES_DEV = 1152
CHANNELS = 64
MLP_WIDTH = 128
RADIAL = 8
SPECIES = 4
DOM_X = 8
DOM_Y = 8
DOM_Z = 8
DOMAINS = 512


def lattice(key):
    domain_keys = jax.random.split(key, DOMAINS)
    return jax.vmap(lambda one_key: jax.random.permutation(one_key, ATOMS_DEV))(domain_keys).astype(jnp.int32)


def inverse_of(order):
    ranks = jnp.arange(ATOMS_DEV, dtype=jnp.int32)
    return jax.vmap(lambda row_ids: jnp.zeros((ATOMS_DEV,), jnp.int32).at[row_ids].set(ranks))(order)


def draw_site_atom(key, part):
    return lattice(key)


def draw_positions(key, part):
    placed = inverse_of(lattice(key))
    key = jax.random.fold_in(key, 3)
    cell_x = placed // (CELLS * LAYERS)
    cell_y = placed // LAYERS % CELLS
    cell_z = placed % LAYERS
    centres = jnp.stack([cell_x, cell_y, cell_z], axis=1).astype(jnp.float32)
    wobble = jax.random.uniform(key, (DOMAINS, 3, ATOMS_DEV), jnp.float32, -0.2, 0.2)
    return (2.0 * (centres + 0.5 + wobble)).astype(jnp.float32)


def edge_lists(key):
    placed = inverse_of(lattice(key))
    edge_key = jax.random.fold_in(key, 101)
    step_key, shuffle_key = jax.random.split(edge_key)
    step_keys = jax.random.split(step_key, DOMAINS * ATOMS_DEV)
    chosen = jax.vmap(lambda one_key: jax.random.permutation(one_key, 26)[:NEIGH])(step_keys)
    chosen = chosen.reshape(DOMAINS, ATOMS_DEV, NEIGH).astype(jnp.int32)
    full_code = chosen + (chosen >= 13).astype(jnp.int32)
    cell_x = (placed // (CELLS * LAYERS))[:, :, None]
    cell_y = (placed // LAYERS % CELLS)[:, :, None]
    cell_z = (placed % LAYERS)[:, :, None]
    target = ((cell_x + full_code // 9) * (CELLS + 2) + cell_y + full_code // 3 % 3) * (LAYERS + 2) + cell_z + full_code % 3
    centers = jnp.broadcast_to(jnp.arange(ATOMS_DEV, dtype=jnp.int32)[None, :, None], (DOMAINS, ATOMS_DEV, NEIGH))
    shuffle_keys = jax.random.split(shuffle_key, DOMAINS)
    shuffled = jax.vmap(lambda one_key: jax.random.permutation(one_key, EDGES_DEV))(shuffle_keys)
    center_out = jnp.take_along_axis(centers.reshape(DOMAINS, EDGES_DEV), shuffled, axis=1)
    other_out = jnp.take_along_axis(target.reshape(DOMAINS, EDGES_DEV), shuffled, axis=1)
    return (center_out.astype(jnp.int32), other_out.astype(jnp.int32))


def draw_edge_center(key, part):
    paired = edge_lists(key)
    return paired[0]


def draw_edge_other(key, part):
    paired = edge_lists(key)
    return paired[1]


def draw_edge_count(key, part):
    key = jax.random.fold_in(key, 11)
    layer_index = jnp.arange(DOMAINS, dtype=jnp.int32) % DOM_Z
    dropped = 2 * EDGES_DEV // 3 * (DOM_Z - 1 - layer_index) // (DOM_Z - 1)
    jitter = jax.random.randint(key, (DOMAINS,), 0, EDGES_DEV // 8 + 1)
    jitter = jnp.where(layer_index < DOM_Z - 1, jitter, 0)
    return (EDGES_DEV - dropped - jitter).astype(jnp.int32)


def place_ends(drawn, key, smallest, high):
    dims = drawn.shape
    index_at = [jax.random.randint(jax.random.fold_in(key, axis), (), 0, dims[axis]) for axis in range(len(dims))]
    drawn = drawn.at[tuple(index_at)].set(smallest)
    longest = dims.index(max(dims))
    index_at[longest] = (index_at[longest] + 1) % dims[longest]
    return drawn.at[tuple(index_at)].set(high)


def normal_values(rng, extent, scale, most, kind=jnp.bfloat16):
    array = scale * jax.random.normal(rng, extent, jnp.float32)
    return jnp.clip(array, min=-most, max=most).astype(kind)


def setup_inputs(seed: int = 0) -> dict:
    keys = jax.random.split(jax.random.key(seed), 14)
    return {
        "positions": draw_positions(jax.random.fold_in(keys[13], 71), 0),
        "species": place_ends(jax.random.randint(keys[1], (DOMAINS, ATOMS_DEV), 0, SPECIES), jax.random.fold_in(keys[1], 1), 0, SPECIES - 1).astype(jnp.int32),
        "site_atom": draw_site_atom(jax.random.fold_in(keys[13], 71), 0),
        "edge_center": draw_edge_center(jax.random.fold_in(keys[13], 71), 0),
        "edge_other": draw_edge_other(jax.random.fold_in(keys[13], 71), 0),
        "edge_count": draw_edge_count(jax.random.fold_in(keys[13], 71), 0),
        "w_in": normal_values(keys[6], (MLP_WIDTH, RADIAL + 2 * SPECIES), (RADIAL + 2 * SPECIES) ** -0.5, 1.5, jnp.float32),
        "w_two": normal_values(keys[7], (CHANNELS, MLP_WIDTH), MLP_WIDTH ** -0.5, 0.5, jnp.float32),
        "w_env": normal_values(keys[8], (CHANNELS, CHANNELS), CHANNELS ** -0.5, 0.75, jnp.float32),
        "w_value": normal_values(keys[9], (CHANNELS, CHANNELS), CHANNELS ** -0.5, 0.75, jnp.float32),
        "w_latent": normal_values(keys[10], (MLP_WIDTH, 4 * CHANNELS), (4 * CHANNELS) ** -0.5, 0.375, jnp.float32),
        "w_out": normal_values(keys[11], (CHANNELS, MLP_WIDTH), MLP_WIDTH ** -0.5, 0.5, jnp.float32),
        "readout": normal_values(keys[12], (CHANNELS,), CHANNELS ** -0.5, 0.75, jnp.float32),
    }


spacing = 2.0
cutoff = 5.0
highest = lax.Precision.HIGHEST

def matmul(left, right):
    return jnp.dot(left, right, precision=highest, preferred_element_type=jnp.float32)

def harmonics(displacement):
    comp_x = displacement[0] / cutoff
    comp_y = displacement[1] / cutoff
    comp_z = displacement[2] / cutoff
    root_three = math.sqrt(3.0)
    return jnp.stack([jnp.ones_like(comp_x), comp_x, comp_y, comp_z, root_three * comp_x * comp_y, root_three * comp_y * comp_z, root_three * comp_x * comp_z, 0.5 * root_three * (comp_x * comp_x - comp_y * comp_y), 0.5 * (2.0 * comp_z * comp_z - comp_x * comp_x - comp_y * comp_y)], axis=0)

def step_table():
    sign_rows = []
    for cell_count in (CELLS, CELLS, LAYERS):
        cell_ids = jnp.arange(cell_count + 2, dtype=jnp.int32)
        upper_side = (cell_ids == cell_count + 1).astype(jnp.float32)
        lower_side = (cell_ids == 0).astype(jnp.float32)
        sign_rows.append(spacing * cell_count * (upper_side - lower_side))
    grid_shape = (CELLS + 2, CELLS + 2, LAYERS + 2)
    return jnp.stack([jnp.broadcast_to(sign_rows[0][:, None, None], grid_shape), jnp.broadcast_to(sign_rows[1][None, :, None], grid_shape), jnp.broadcast_to(sign_rows[2][None, None, :], grid_shape)], axis=0).reshape(3, -1)

def domain_energy(local_pos, extended_pos, local_kind, extended_kind, center, partner, live_count, weights):
    w_in, w_two, w_env, w_value, w_latent, w_out, readout = weights
    atom_count = local_pos.shape[1]
    edge_total = center.shape[0]
    channels = w_env.shape[0]
    displacement = jnp.take(extended_pos, partner, axis=1) - jnp.take(local_pos, center, axis=1)
    scaled_sq = lax.optimization_barrier(jnp.sum(displacement * displacement, axis=0)) / (cutoff * cutoff)
    envelope = (1.0 - scaled_sq) * (1.0 - scaled_sq)
    live_mask = (jnp.arange(edge_total, dtype=jnp.int32) < live_count).astype(jnp.float32)
    orders = jnp.arange(RADIAL, dtype=jnp.int32).astype(jnp.float32)[:, None]
    radial = jnp.cos(math.pi * orders * scaled_sq[None, :])
    species_ids = jnp.arange(SPECIES, dtype=jnp.int32)[:, None]
    center_kind = (jnp.take(local_kind, center)[None, :] == species_ids).astype(jnp.float32)
    partner_kind = (jnp.take(extended_kind, partner)[None, :] == species_ids).astype(jnp.float32)
    inputs = jnp.concatenate([radial, center_kind, partner_kind], axis=0)
    two_body = matmul(w_two, jax.nn.silu(matmul(w_in, inputs)))
    weight_env = matmul(w_env, two_body) * (envelope * live_mask)[None, :]
    values = matmul(w_value, two_body)
    harmonic = harmonics(displacement)
    outer_terms = (harmonic[:, None, :] * weight_env[None, :, :]).reshape(9 * channels, edge_total)
    environment = jnp.zeros((9 * channels, atom_count), jnp.float32).at[:, center].add(outer_terms)
    at_edges = jnp.take(environment, center, axis=1).reshape(9, channels, edge_total) * harmonic[:, None, :]
    path_zero = at_edges[0]
    path_one = at_edges[1] + at_edges[2] + at_edges[3]
    path_two = at_edges[4] + at_edges[5] + at_edges[6] + at_edges[7] + at_edges[8]
    latent_in = jnp.concatenate([two_body, path_zero * values, path_one * values, path_two * values], axis=0)
    latent = matmul(w_out, jax.nn.silu(matmul(w_latent, latent_in)))
    edge_energy = matmul(readout, latent) * envelope * live_mask
    return jnp.zeros((atom_count,), jnp.float32).at[center].add(edge_energy)

def axis_map(coord, domain_count, cell_count):
    cell_ids = jnp.arange(cell_count + 2, dtype=jnp.int32)
    global_ids = (coord[:, None] * cell_count + cell_ids[None, :] - 1) % (domain_count * cell_count)
    return (global_ids // cell_count, global_ids % cell_count)

def reference(positions, species, site_atom, edge_center, edge_other, edge_count, w_in, w_two, w_env, w_value, w_latent, w_out, readout):
    domain_ids = jnp.arange(DOMAINS, dtype=jnp.int32)
    coord_x = domain_ids // (DOM_Y * DOM_Z)
    coord_y = domain_ids // DOM_Z % DOM_Y
    coord_z = domain_ids % DOM_Z
    owner_x, local_x = axis_map(coord_x, DOM_X, CELLS)
    owner_y, local_y = axis_map(coord_y, DOM_Y, CELLS)
    owner_z, local_z = axis_map(coord_z, DOM_Z, LAYERS)
    owner_dom = ((owner_x[:, :, None, None] * DOM_Y + owner_y[:, None, :, None]) * DOM_Z + owner_z[:, None, None, :]).reshape(DOMAINS, -1)
    site_ids = ((local_x[:, :, None, None] * CELLS + local_y[:, None, :, None]) * LAYERS + local_z[:, None, None, :]).reshape(DOMAINS, -1)
    atom_ids = site_atom[owner_dom, site_ids]
    gathered = positions[owner_dom, :, atom_ids]
    extended_pos = jnp.moveaxis(gathered, 2, 1) + step_table()[None]
    extended_kind = species[owner_dom, atom_ids]
    weights = (w_in, w_two, w_env, w_value, w_latent, w_out, readout)

    def per_domain(operands):
        local_pos, remote_pos, local_kind, remote_kind, center, partner, live_count = operands

        def energy_of(first, second):
            return domain_energy(first, second, local_kind, remote_kind, center, partner, live_count, weights)
        site_part, pullback = jax.vjp(energy_of, local_pos, remote_pos)
        g_local, g_extended = pullback(jnp.ones_like(site_part))
        virial_part = -(matmul(local_pos, g_local.T) + matmul(remote_pos, g_extended.T))
        return (site_part, g_local, g_extended, virial_part)
    site_energy, g_local, g_extended, virial_parts = lax.map(per_domain, (positions, extended_pos, species, extended_kind, edge_center, edge_other, edge_count))
    summed = g_local.at[owner_dom, :, atom_ids].add(jnp.moveaxis(g_extended, 1, 2))
    forces = -summed
    normalizer = 1.0 / math.sqrt(EDGES_DEV * DOMAINS)
    virial = lax.optimization_barrier(jnp.sum(virial_parts, axis=0)) * normalizer
    return (forces, site_energy, virial)
```

```python
import math

import jax
import jax.numpy as jnp
import numpy as np
from jax import lax
from jax.experimental import pallas as pl
from jax.experimental.pallas import tpu as pltpu
from jax.sharding import PartitionSpec as P

CELLS = 6
LAYERS = 2
ATOMS = 72
EDGES = 1152
BLOCKS = 9
LANES = 128
MAIN = 64
COUNT = 8
F32 = jnp.float32
BF16 = jnp.bfloat16
HIGHEST = lax.Precision.HIGHEST
ROOT3 = math.sqrt(3.0)
RING = 28
STEPS = [(dx, dy) for dx in (-1, 0, 1) for dy in (-1, 0, 1) if (dx, dy) != (0, 0)]


RIM_SITES = (
    [(0, y) for y in range(6)]
    + [(5, y) for y in range(6)]
    + [(x, 0) for x in range(1, 5)]
    + [(x, 5) for x in range(1, 5)]
)


def ring_index(i, j):
    if i == 0:
        return j
    if i == 7:
        return 8 + j
    if j == 0:
        return 16 + i - 1
    return 22 + i - 1


def cell_number(i, j, k):
    if i in (0, 7) or j in (0, 7):
        return k * RING + ring_index(i, j)
    return 112 + k * 36 + (i - 1) * 6 + (j - 1)


def tables():
    forward = np.zeros((10 * LANES, 256), np.float32)
    for n, (dx, dy) in enumerate(STEPS):
        for m, (x, y) in enumerate(RIM_SITES):
            i = {0: x + 1, 1: 7 if x == 0 else None, -1: 0 if x == 5 else None}[dx]
            j = {0: y + 1, 1: 7 if y == 0 else None, -1: 0 if y == 5 else None}[dy]
            if i is None or j is None:
                continue
            for k in range(4):
                forward[n * LANES + k * 32 + m, cell_number(i, j, k)] = 1.0
    for x in range(CELLS):
        for y in range(CELLS):
            for k, at in ((0, 0), (3, 64), (1, LANES), (2, LANES + 64)):
                forward[8 * LANES + at + x * 6 + y, cell_number(x + 1, y + 1, k)] = 1.0
    back = np.zeros((10 * LANES, 256), np.float32)
    places = {0: 0, 3: 64, 1: LANES, 2: LANES + 64}
    for n, (dx, dy) in enumerate(STEPS):
        for i in range(8):
            for j in range(8):
                if not (i in (0, 7) or j in (0, 7)):
                    continue
                x, y = dx * 6 + i - 1, dy * 6 + j - 1
                if 0 <= x < 6 and 0 <= y < 6:
                    for k in range(4):
                        back[n * LANES + cell_number(i, j, k), places[k] + x * 6 + y] = 1.0
    for x in range(CELLS):
        for y in range(CELLS):
            for k in range(4):
                back[8 * LANES + cell_number(x + 1, y + 1, k), places[k] + x * 6 + y] = 1.0
    return forward, back


FORWARD, BACK = tables()


def parts_of(x, count):
    found = []
    for _ in range(count - 1):
        part = x.astype(BF16).astype(F32)
        found.append(part)
        x = x - part
    found.append(x)
    return found


def split_rows(x, count):
    return jnp.concatenate(parts_of(x, count), axis=0).astype(BF16)


def exact_dot(x, table, count=3):
    rows = x.shape[0]
    out = jnp.dot(split_rows(x, count), table, preferred_element_type=F32)
    return sum(out[i * rows : (i + 1) * rows] for i in range(1, count)) + out[:rows]


def exact_dot_nt(x, table, count=3):
    rows = x.shape[0]
    out = lax.dot_general(split_rows(x, count), table, (((1,), (1,)), ((), ())), preferred_element_type=F32)
    return sum(out[i * rows : (i + 1) * rows] for i in range(1, count)) + out[:rows]


def pad_rows(x):
    return jnp.concatenate([x, jnp.zeros((8 - x.shape[0], x.shape[1]), F32)], axis=0)


def iota(shape, dim):
    return lax.broadcasted_iota(jnp.int32, shape, dim)


def as_hot(mask):
    return jnp.where(mask, 1.0, 0.0).astype(BF16)


def fetch(sources, buffers, sems):
    copies = [pltpu.make_async_copy(src, dst, sems.at[n]) for n, (src, dst) in enumerate(zip(sources, buffers))]
    for copy in copies:
        copy.start()
    for copy in copies:
        copy.wait()


def atom_rows(pos_ref, kind_ref):
    kind = kind_ref[...].astype(F32)
    return jnp.concatenate([pos_ref[0], pos_ref[1], pos_ref[2], kind, jnp.zeros((4, ATOMS), F32)], axis=0)


def lane_sites():
    lane = iota((8, 3 * LANES), 1)
    part, at = lane >> 7, lane & 63
    second = (lane & 64) > 0
    rim = jnp.where(
        at < 12,
        jnp.where(at < 6, at, 24 + at),
        jnp.where(at < 16, 6 * (at - 11), 6 * (at - 15) + 5),
    )
    whole = jnp.where(at < 36, at, 1000)
    rim = jnp.where(at < 20, rim, 1000)
    layer = jnp.where(part == 0, jnp.where(second, 1, 0), part - 1)
    return 2 * jnp.where((part > 0) & second, rim, whole) + layer


def send_kernel(pos_hbm, kind_hbm, site_hbm, own_ref, down_ref, up_ref, hot_ref, pos_ref, kind_ref, site_ref, sems):
    fetch((pos_hbm, kind_hbm, site_hbm), (pos_ref, kind_ref, site_ref), sems)
    rows = atom_rows(pos_ref, kind_ref)
    hot = as_hot(iota((ATOMS, ATOMS), 0) == site_ref[...])
    pick = as_hot(iota((ATOMS, 3 * LANES), 0) == lane_sites()[0:1])
    placed = jnp.dot(hot, pick, preferred_element_type=F32).astype(BF16)
    out = exact_dot(rows, placed)
    own_ref[...] = out[:4, 0:LANES]
    down_ref[...] = out[:4, LANES : 2 * LANES]
    up_ref[...] = out[:4, 2 * LANES : 3 * LANES]
    hot_ref[...] = placed[:, 0:LANES]


def column_kernel(down_ref, up_ref, below_ref, above_ref, tie_ref, msg_ref, outer_ref):
    lane = lax.broadcasted_iota(jnp.int32, (8, LANES), 1)

    def rim(x, at):
        return pltpu.roll(x, (at - 64) % LANES, 1)

    below, above, low, high = (pad_rows(ref[...]) for ref in (below_ref, above_ref, down_ref, up_ref))
    msg = jnp.where(
        lane < 32,
        rim(below, 0),
        jnp.where(lane < 64, rim(low, 32), jnp.where(lane < 96, rim(high, 64), rim(above, 96))),
    )
    outer_ref[...] = jnp.where(lane < 64, below, pltpu.roll(above, 64, 1))[:4]
    msg_ref[...] = jnp.broadcast_to(msg[:4][None], (COUNT * COUNT, 4, LANES))


def cat_of(w):
    high = w.astype(BF16).astype(F32)
    low = w - high
    return jnp.concatenate([high, high, low], axis=1).astype(BF16)


def cell_shifts():
    lane = iota((8, 256), 1)
    row = iota((8, 256), 0)
    inside = lane - 112
    ring_layer = jnp.where(lane >= 28, 1, 0) + jnp.where(lane >= 56, 1, 0) + jnp.where(lane >= 84, 1, 0)
    ring = lane - 28 * ring_layer
    outer = lane < 112
    layer = jnp.where(
        outer,
        ring_layer,
        jnp.where(inside >= 36, 1, 0) + jnp.where(inside >= 72, 1, 0) + jnp.where(inside >= 108, 1, 0),
    )
    low_z = layer == 0
    high_z = layer == 3
    corner_low = (ring == 0) | (ring == 8)
    corner_high = (ring == 7) | (ring == 15)
    low_y = outer & (corner_low | ((ring >= 16) & (ring < 22)))
    high_y = outer & (corner_high | (ring >= 22))
    low_x = outer & (ring < 8)
    high_x = outer & (ring >= 8) & (ring < 16)

    def sides(low, high, edge):
        return jnp.where(high, edge, 0.0) - jnp.where(low, edge, 0.0)

    return jnp.where(
        row == 0,
        sides(low_x, high_x, 12.0),
        jnp.where(row == 1, sides(low_y, high_y, 12.0), jnp.where(row == 2, sides(low_z, high_z, 4.0), 0.0)),
    )


def prepare_kernel(count_ref, *refs):
    sources, outputs, buffers, sems = refs[:13], refs[13:26], refs[26:37], refs[37]
    cell_ref, live_ref, own_ref, shift_ref = outputs[:4]
    win_ref, w3_ref, wlat_ref, wlat_t_ref, w3_t_ref, win_t_ref, read_ref = outputs[4:11]
    fetch(sources, buffers + outputs[11:], sems)
    center_ref, other_ref, pos_ref, kind_ref, w_in_ref, w_two_ref, w_env_ref = buffers[:7]
    w_value_ref, w_latent_ref, w_out_ref, readout_ref = buffers[7:]
    shift_ref[...] = cell_shifts()
    before = as_hot((iota((LANES, 256), 0) < iota((LANES, 256), 1)) | (iota((LANES, 256), 1) >= LANES))
    lane = iota((ATOMS, 256), 1)
    spread = as_hot(iota((ATOMS, 256), 0) == jnp.where(lane < LANES, lane & 63, MAIN + (lane & 7)))
    center = center_ref[...]
    other = other_ref[...]
    atom = lax.broadcasted_iota(jnp.int32, (ATOMS, EDGES), 0)
    hot = jnp.where(atom == center, 1.0, 0.0)
    hot16 = hot.astype(BF16)
    running = jnp.zeros((ATOMS, LANES), F32)
    ranks = []
    for b in range(BLOCKS):
        at = slice(b * LANES, (b + 1) * LANES)
        sums = jnp.dot(hot16[:, at], before, preferred_element_type=F32)
        ranks.append(jnp.sum(hot[:, at] * (sums[:, :LANES] + running), axis=0, keepdims=True))
        running = running + sums[:, LANES:]
    rank = jnp.concatenate(ranks, axis=1).astype(jnp.int32)
    is_main = center < MAIN
    block = jnp.where(is_main, rank >> 1, BLOCKS - 1)
    lane = jnp.where(is_main, (rank & 1) * MAIN + center, rank * 8 + (center - MAIN))
    i, j, k = other >> 5, (other >> 2) & 7, other & 3
    ring = jnp.where(
        i == 0, j, jnp.where(i == 7, 8 + j, jnp.where(j == 0, 15 + i, jnp.where(j == 7, 21 + i, -1)))
    )
    cell = jnp.where(ring >= 0, k * RING + ring, 112 + k * 36 + (i - 1) * 6 + (j - 1)).astype(F32)
    slot = lax.broadcasted_iota(jnp.int32, (1, EDGES), 1)
    live = jnp.where(slot < count_ref[0], 1.0, 0.0)
    row = lax.broadcasted_iota(jnp.int32, (16, EDGES), 0)
    left = jnp.concatenate([jnp.where(row == block, cell, 0.0), jnp.where(row == block, live, 0.0)], axis=0)
    lane_hot = jnp.where(lax.broadcasted_iota(jnp.int32, (LANES, EDGES), 0) == lane, 1.0, 0.0).astype(BF16)
    placed = lax.dot_general(
        left.astype(BF16), lane_hot, (((1,), (1,)), ((), ())), preferred_element_type=F32
    )
    for b in range(BLOCKS):
        at = slice(b * LANES, (b + 1) * LANES)
        cell_ref[:, at] = placed[b : b + 1].astype(jnp.int32)
        live_ref[:, at] = placed[16 + b : 17 + b]
    own_ref[...] = exact_dot(atom_rows(pos_ref, kind_ref), spread)

    w_in_t = w_in_ref[...]
    win_ref[...] = cat_of(w_in_t.T)
    w_two = w_two_ref[...]
    mixed = jnp.concatenate([w_env_ref[...], w_value_ref[...]], axis=0)
    w3 = jnp.concatenate(
        [w_two, jnp.dot(mixed, w_two, precision=HIGHEST, preferred_element_type=F32)], axis=0
    )
    w3_ref[...] = cat_of(w3)
    w3_t_ref[...] = cat_of(w3.T)
    w_latent = w_latent_ref[...]
    wlat_ref[...] = cat_of(w_latent)
    wlat_t_ref[...] = cat_of(w_latent.T)
    win_t_ref[...] = cat_of(w_in_t)
    square = lax.broadcasted_iota(jnp.int32, (64, 64), 0) == lax.broadcasted_iota(jnp.int32, (64, 64), 1)
    column = jnp.sum(jnp.where(square, readout_ref[...], 0.0), axis=1, keepdims=True)
    read_ref[...] = jnp.dot(
        w_out_ref[...].T,
        jnp.broadcast_to(column, (64, LANES)),
        precision=HIGHEST,
        preferred_element_type=F32,
    )


def cos_sin_pi(t):
    whole = jnp.floor(t + 0.5)
    f = t - whole
    half = whole * 0.5
    sign = 1.0 - 4.0 * (half - jnp.floor(half))
    a = f * math.pi
    q = a * a
    c = 1.0 + q * (
        -0.5
        + q * (1 / 24 + q * (-1 / 720 + q * (1 / 40320 + q * (-1 / 3628800 + q * (1 / 479001600)))))
    )
    s = a * (
        1.0
        + q
        * (-1 / 6 + q * (1 / 120 + q * (-1 / 5040 + q * (1 / 362880 + q * (-1 / 39916800 + q * (1 / 6227020800))))))
    )
    return c * sign, s * sign


def sum_slots(main, last):
    main = main + pltpu.roll(main, 64, 1)
    for shift in (64, 32, 16, 8):
        last = last + pltpu.roll(last, shift, 1)
    return main, last


def store_cat(ref, row, depth, at, x):
    high = x.astype(BF16)
    low = (x - high.astype(F32)).astype(BF16)
    ref[pl.ds(pl.multiple_of(row, 16), 16), at] = high
    ref[pl.ds(pl.multiple_of(depth + row, 16), 16), at] = low
    ref[pl.ds(pl.multiple_of(2 * depth + row, 16), 16), at] = high


def neighbour(n):
    dx, dy = STEPS[n]
    gx = lax.axis_index("gx")
    gy = lax.axis_index("gy")
    return lax.rem(gx + (dx + COUNT), COUNT) * COUNT + lax.rem(gy + (dy + COUNT), COUNT)


def main_kernel(
    recv_ref,
    outer_ref,
    inner_ref,
    cell_ref,
    live_ref,
    own_ref,
    shift_ref,
    win_ref,
    w3_ref,
    wlat_ref,
    wlat_t_ref,
    w3_t_ref,
    win_t_ref,
    read_ref,
    forward_ref,
    msg_ref,
    ext_ref,
    local_ref,
    energy_ref,
    hot,
    harm,
    env_live,
    pre,
    slope,
    cat_a,
    cat_b,
    mixed,
    paths,
    environment,
    grad_lat,
    grad_harm,
    grad_env,
    energy,
):
    blocks = [slice(b * LANES, (b + 1) * LANES) for b in range(BLOCKS)]

    columns = [recv_ref[neighbour(n)] for n in range(8)] + [outer_ref[...], inner_ref[...]]
    arrived = pad_rows(jnp.concatenate(columns, axis=1))
    extended = exact_dot(arrived, forward_ref[...]) + shift_ref[...]
    cells = lax.broadcasted_iota(jnp.int32, (256, EDGES), 0)
    hot[...] = jnp.where(cells == cell_ref[...], 1.0, 0.0).astype(BF16)
    partner = exact_dot(extended, hot[...])
    own = own_ref[...]
    center = jnp.concatenate([own[:, :LANES]] * 8 + [own[:, LANES:]], axis=1)
    displacement = partner - center

    def wide(x, row):
        return jnp.broadcast_to(x[row : row + 1], (8, EDGES))

    x = wide(displacement, 0) * 0.2
    y = wide(displacement, 1) * 0.2
    z = wide(displacement, 2) * 0.2
    scaled = x * x + y * y + z * z
    live = jnp.broadcast_to(live_ref[...], (8, EDGES))
    env_live[...] = (1.0 - scaled) * (1.0 - scaled) * live
    harm[0] = x
    harm[1] = y
    harm[2] = z
    harm[3] = ROOT3 * x * y
    harm[4] = ROOT3 * y * z
    harm[5] = ROOT3 * x * z
    harm[6] = (0.5 * ROOT3) * (x * x - y * y)
    harm[7] = 0.5 * (2.0 * z * z - x * x - y * y)

    order = lax.broadcasted_iota(jnp.int32, (8, EDGES), 0)
    orders = order.astype(F32)
    radial, radial_sin = cos_sin_pi(orders * scaled)
    kinds = jnp.where(order < 4, wide(center, 3), wide(partner, 3) + 4.0)
    one_hot = jnp.where(kinds == orders, 1.0, 0.0)
    inputs = jnp.concatenate([radial, one_hot], axis=0)
    inputs_high = inputs.astype(BF16)
    inputs_low = (inputs - inputs_high.astype(F32)).astype(BF16)
    pre[0:16] = jnp.dot(
        win_ref[...],
        jnp.concatenate([inputs_high, inputs_low, inputs_high], axis=0),
        preferred_element_type=F32,
    ).reshape(16, 8, EDGES)

    def first_layer(c, carry):
        v = pre[pl.ds(2 * c, 2)]
        gate = 1.0 / (1.0 + jnp.exp(-v))
        out = v * gate
        slope[pl.ds(2 * c, 2)] = gate + out * (1.0 - gate)
        store_cat(cat_a, 16 * c, 128, slice(None), out.reshape(16, EDGES))
        return carry

    lax.fori_loop(0, 8, first_layer, 0)
    mixed[...] = jnp.dot(w3_ref[...], cat_a[0:384], preferred_element_type=F32).reshape(24, 8, EDGES)

    def forward_tile(t, carry):
        sums = [[None, None] for _ in range(9)]
        for b, at in enumerate(blocks):
            weight = mixed[pl.ds(8 + 2 * t, 2), :, at] * env_live[:, at]
            part = 0 if b < 8 else 1
            for r in range(9):
                term = weight if r == 0 else weight * harm[r - 1, :, at]
                sums[r][part] = term if sums[r][part] is None else sums[r][part] + term
        found = []
        for r in range(9):
            main, last = sum_slots(sums[r][0].reshape(16, LANES), sums[r][1].reshape(16, LANES))
            main, last = main.reshape(2, 8, LANES), last.reshape(2, 8, LANES)
            environment[r, pl.ds(2 * t, 2), :, 0:LANES] = main
            environment[r, pl.ds(2 * t, 2), :, LANES : 2 * LANES] = last
            found.append((main, last))
        for b, at in enumerate(blocks):
            part = 0 if b < 8 else 1
            h = [None] + [harm[r, :, at] for r in range(8)]
            e = [found[r][part] for r in range(9)]
            one = h[1] * e[1] + h[2] * e[2] + h[3] * e[3]
            two = h[4] * e[4] + h[5] * e[5] + h[6] * e[6] + h[7] * e[7] + h[8] * e[8]
            paths[0, pl.ds(2 * t, 2), :, at] = one
            paths[1, pl.ds(2 * t, 2), :, at] = two
            values = mixed[pl.ds(16 + 2 * t, 2), :, at]
            base = 16 * t
            store_cat(cat_b, base, 256, at, mixed[pl.ds(2 * t, 2), :, at].reshape(16, LANES))
            store_cat(cat_b, 64 + base, 256, at, (e[0] * values).reshape(16, LANES))
            store_cat(cat_b, 128 + base, 256, at, (one * values).reshape(16, LANES))
            store_cat(cat_b, 192 + base, 256, at, (two * values).reshape(16, LANES))
        return carry

    lax.fori_loop(0, 4, forward_tile, 0)
    pre[...] = jnp.dot(wlat_ref[...], cat_b[...], preferred_element_type=F32).reshape(16, 8, EDGES)
    energy[...] = jnp.zeros((8, EDGES), F32)

    def second_layer(c, carry):
        v = pre[pl.ds(2 * c, 2)]
        gate = 1.0 / (1.0 + jnp.exp(-v))
        out = v * gate
        weights = read_ref[pl.ds(pl.multiple_of(16 * c, 16), 16), :].reshape(2, 8, LANES)
        weights = jnp.concatenate([weights] * BLOCKS, axis=2)
        product = weights * out
        energy[...] += product[0] + product[1]
        back = weights * (gate + out * (1.0 - gate)) * env_live[...]
        store_cat(cat_a, 16 * c, 128, slice(None), back.reshape(16, EDGES))
        return carry

    lax.fori_loop(0, 8, second_layer, 0)
    grad_lat[...] = jnp.dot(wlat_t_ref[...], cat_a[...], preferred_element_type=F32).reshape(32, 8, EDGES)
    grad_harm[...] = jnp.zeros((8, 8, EDGES), F32)
    grad_env[...] = jnp.zeros((8, EDGES), F32)

    def backward_tile(t, carry):
        base = 16 * t
        sums = [[None, None] for _ in range(9)]
        for b, at in enumerate(blocks):
            part = 0 if b < 8 else 1
            lanes = slice(part * LANES, (part + 1) * LANES)
            values = mixed[pl.ds(16 + 2 * t, 2), :, at]
            d = [grad_lat[pl.ds(8 + 8 * l + 2 * t, 2), :, at] for l in range(3)]
            zero = environment[0, pl.ds(2 * t, 2), :, lanes]
            one = paths[0, pl.ds(2 * t, 2), :, at]
            two = paths[1, pl.ds(2 * t, 2), :, at]
            d_values = d[0] * zero + d[1] * one + d[2] * two
            store_cat(cat_b, 128 + base, 192, at, d_values.reshape(16, LANES))
            store_cat(cat_b, base, 192, at, grad_lat[pl.ds(2 * t, 2), :, at].reshape(16, LANES))
            q = [d[l] * values for l in range(3)]
            for r in range(9):
                level = 0 if r == 0 else (1 if r < 4 else 2)
                term = q[0] if r == 0 else q[level] * harm[r - 1, :, at]
                sums[r][part] = term if sums[r][part] is None else sums[r][part] + term
        found = []
        for r in range(9):
            main, last = sum_slots(sums[r][0].reshape(16, LANES), sums[r][1].reshape(16, LANES))
            found.append((main.reshape(2, 8, LANES), last.reshape(2, 8, LANES)))
        for b, at in enumerate(blocks):
            part = 0 if b < 8 else 1
            lanes = slice(part * LANES, (part + 1) * LANES)
            raw = mixed[pl.ds(8 + 2 * t, 2), :, at]
            envelope = env_live[:, at]
            weight = raw * envelope
            values = mixed[pl.ds(16 + 2 * t, 2), :, at]
            q = [None] + [grad_lat[pl.ds(8 + 8 * l + 2 * t, 2), :, at] * values for l in (1, 2)]
            d_weight = found[0][part]
            for r in range(1, 9):
                g = found[r][part]
                d_weight = d_weight + harm[r - 1, :, at] * g
                level = 1 if r < 4 else 2
                term = q[level] * environment[r, pl.ds(2 * t, 2), :, lanes] + weight * g
                grad_harm[r - 1, :, at] += term[0] + term[1]
            slack = d_weight * raw
            grad_env[:, at] += slack[0] + slack[1]
            store_cat(cat_b, 64 + base, 192, at, (d_weight * envelope).reshape(16, LANES))
        return carry

    lax.fori_loop(0, 4, backward_tile, 0)
    pre[...] = jnp.dot(w3_t_ref[...], cat_b[0:576], preferred_element_type=F32).reshape(16, 8, EDGES)

    def first_back(c, carry):
        back = pre[pl.ds(2 * c, 2)] * slope[pl.ds(2 * c, 2)]
        store_cat(cat_a, 16 * c, 128, slice(None), back.reshape(16, EDGES))
        return carry

    lax.fori_loop(0, 8, first_back, 0)
    d_radial = jnp.dot(win_t_ref[...], cat_a[...], preferred_element_type=F32)[:8]

    x, y, z = harm[0], harm[1], harm[2]
    scaled = x * x + y * y + z * z
    live = jnp.broadcast_to(live_ref[...], (8, EDGES))
    d_scaled = d_radial * (orders * radial_sin) * (-math.pi) + (grad_env[...] + energy[...]) * (
        -2.0 * (1.0 - scaled) * live
    )
    g = [grad_harm[r] for r in range(8)]
    twice = 2.0 * d_scaled
    d_x = g[0] + ROOT3 * (y * g[3] + z * g[5] + x * g[6]) - x * g[7] + twice * x
    d_y = g[1] + ROOT3 * (x * g[3] + z * g[4] - y * g[6]) - y * g[7] + twice * y
    d_z = g[2] + ROOT3 * (y * g[4] + x * g[5]) + 2.0 * z * g[7] + twice * z
    e = energy[...] * env_live[...]
    rows = [jnp.sum(v, axis=0, keepdims=True) for v in (d_x * 0.2, d_y * 0.2, d_z * 0.2, e)]
    grads = jnp.concatenate(rows + [jnp.zeros((4, EDGES), F32)], axis=0)

    def over_blocks(v):
        total = v[:, blocks[0]]
        for b in range(1, 8):
            total = total + v[:, blocks[b]]
        return total

    main, last = sum_slots(over_blocks(grads), grads[:, blocks[8]])
    atoms = jnp.concatenate([main[:, :MAIN], last[:, : ATOMS - MAIN]], axis=1)
    local_ref[...] = atoms
    energy_ref[...] = atoms[3:4]

    extended_grad = exact_dot_nt(grads, hot[...])
    ext_ref[...] = extended_grad[:4]
    lane = lax.broadcasted_iota(jnp.int32, (8, LANES), 1)
    row = lax.broadcasted_iota(jnp.int32, (8, LANES), 0)
    virial = jnp.zeros((8, LANES), F32)
    for a, comp in enumerate((x, y, z)):
        product = comp * grads
        total = jnp.sum(over_blocks(product) + product[:, blocks[8]], axis=1, keepdims=True)
        virial = jnp.where((lane == row + 3 * a) & (row < 3), total * 5.0, virial)
    virial = jnp.sum(virial, axis=0, keepdims=True)
    message = jnp.concatenate([extended_grad[:3, :LANES], virial], axis=0)
    msg_ref[...] = jnp.broadcast_to(message[None], (COUNT * COUNT, 4, LANES))


def middle_kernel(recv_ref, ext_ref, back_ref, msg_ref, keep_ref):
    columns = [recv_ref[neighbour(n)] for n in range(8)] + [ext_ref[...]]
    arrived = pad_rows(jnp.concatenate(columns, axis=1))
    sums = exact_dot(arrived, back_ref[...])
    total = jnp.sum(recv_ref[...], axis=0)
    message = jnp.concatenate([sums[:3, :LANES], total[3:4]], axis=0)
    msg_ref[...] = jnp.broadcast_to(message[None], (COUNT, 4, LANES))
    keep_ref[...] = sums[:, LANES:]


def last_kernel(recv_ref, keep_ref, local_ref, hot_ref, force_ref, virial_ref):
    gz = lax.axis_index("gz")
    above = pad_rows(recv_ref[lax.rem(gz + 1, COUNT)])
    below = pad_rows(recv_ref[lax.rem(gz + (COUNT - 1), COUNT)])
    lane = lax.broadcasted_iota(jnp.int32, (8, LANES), 1)
    row = lax.broadcasted_iota(jnp.int32, (8, LANES), 0)
    sites = keep_ref[...] + jnp.where(lane < 64, pltpu.roll(below, 64, 1), pltpu.roll(above, 64, 1))
    atoms = exact_dot_nt(sites, hot_ref[...])
    force = local_ref[...] - atoms
    for comp in range(3):
        force_ref[comp] = force[comp : comp + 1]
    total = jnp.broadcast_to(jnp.sum(recv_ref[...], axis=0)[3:4], (8, LANES))
    normalizer = -1.0 / math.sqrt(EDGES * COUNT * COUNT * COUNT)
    virial = jnp.zeros((8, LANES), F32)
    for b in range(3):
        entry = jnp.sum(jnp.where(lane == 3 * row + b, total, 0.0), axis=1, keepdims=True)
        virial = jnp.where(lane == b, entry * normalizer, virial)
    virial_ref[...] = virial[:3, :3]


def shape(*dims, dtype=F32):
    return jax.ShapeDtypeStruct(dims, dtype)


def in_hbm(*arrays):
    return [pltpu.with_memory_space_constraint(x, pltpu.HBM) for x in arrays]


def params():
    return pltpu.CompilerParams(vmem_limit_bytes=48 * 1024 * 1024)


def body(
    positions,
    species,
    site_atom,
    edge_center,
    edge_other,
    edge_count,
    w_in,
    w_two,
    w_env,
    w_value,
    w_latent,
    w_out,
    readout,
):
    half = (4, LANES)
    hbm = pl.BlockSpec(memory_space=pltpu.HBM)
    smem = pl.BlockSpec(memory_space=pltpu.SMEM)
    columns_first = jnp.transpose(positions, (1, 0, 2))
    own, down, up, hot = pl.pallas_call(
        send_kernel,
        in_specs=[hbm] * 3,
        out_shape=(shape(*half), shape(*half), shape(*half), shape(ATOMS, LANES, dtype=BF16)),
        scratch_shapes=[
            pltpu.VMEM((3, 1, ATOMS), F32),
            pltpu.VMEM((1, ATOMS), jnp.int32),
            pltpu.VMEM((1, ATOMS), jnp.int32),
            pltpu.SemaphoreType.DMA((3,)),
        ],
        compiler_params=params(),
        name="sites",
    )(*in_hbm(columns_first, species, site_atom))
    ahead = [(i, (i + 1) % COUNT) for i in range(COUNT)]
    behind = [(target, source) for source, target in ahead]
    below = lax.ppermute(up, "gz", ahead)
    above = lax.ppermute(down, "gz", behind)

    inputs = (
        edge_center,
        edge_other,
        columns_first,
        species,
        w_in.T,
        w_two,
        w_env,
        w_value,
        w_latent,
        w_out,
        readout.reshape(1, 64),
    )
    routes = (jnp.asarray(FORWARD, BF16), jnp.asarray(BACK, BF16))
    prepared = pl.pallas_call(
        prepare_kernel,
        in_specs=[smem] + [hbm] * (len(inputs) + 2),
        out_shape=(
            shape(1, EDGES, dtype=jnp.int32),
            shape(1, EDGES),
            shape(8, 256),
            shape(8, 256),
            shape(128, 48, dtype=BF16),
            shape(192, 384, dtype=BF16),
            shape(128, 768, dtype=BF16),
            shape(256, 384, dtype=BF16),
            shape(128, 576, dtype=BF16),
            shape(16, 384, dtype=BF16),
            shape(128, LANES),
            shape(10 * LANES, 256, dtype=BF16),
            shape(10 * LANES, 256, dtype=BF16),
        ),
        scratch_shapes=[pltpu.VMEM(x.shape, x.dtype) for x in inputs] + [pltpu.SemaphoreType.DMA((len(inputs) + 2,))],
        compiler_params=params(),
        cost_estimate=pl.CostEstimate(flops=10_000_000, bytes_accessed=2_000_000, transcendentals=0),
        name="slots_and_weights",
    )(edge_count, *in_hbm(*inputs, *routes))

    planes = (COUNT * COUNT, 4, LANES)
    column, outer = pl.pallas_call(
        column_kernel,
        out_shape=(shape(*planes), shape(*half)),
        compiler_params=params(),
        name="column",
    )(down, up, below, above, prepared[3])
    arrived = lax.all_to_all(column, ("gx", "gy"), 0, 0)

    message, extended_grad, local_grad, site_energy = pl.pallas_call(
        main_kernel,
        out_shape=(shape(*planes), shape(4, 256), shape(8, ATOMS), shape(1, ATOMS)),
        scratch_shapes=[
            pltpu.VMEM((256, EDGES), BF16),
            pltpu.VMEM((8, 8, EDGES), F32),
            pltpu.VMEM((8, EDGES), F32),
            pltpu.VMEM((16, 8, EDGES), F32),
            pltpu.VMEM((16, 8, EDGES), F32),
            pltpu.VMEM((384, EDGES), BF16),
            pltpu.VMEM((768, EDGES), BF16),
            pltpu.VMEM((24, 8, EDGES), F32),
            pltpu.VMEM((2, 8, 8, EDGES), F32),
            pltpu.VMEM((9, 8, 8, 256), F32),
            pltpu.VMEM((32, 8, EDGES), F32),
            pltpu.VMEM((8, 8, EDGES), F32),
            pltpu.VMEM((8, EDGES), F32),
            pltpu.VMEM((8, EDGES), F32),
        ],
        compiler_params=params(),
        name="edges",
    )(arrived, outer, own, *prepared[:12])
    returned = lax.all_to_all(message, ("gx", "gy"), 0, 0)
    layers, keep = pl.pallas_call(
        middle_kernel,
        out_shape=(shape(COUNT, 4, LANES), shape(8, LANES)),
        compiler_params=params(),
        name="columns_back",
    )(returned, extended_grad, prepared[12])
    closing = lax.all_to_all(layers, "gz", 0, 0)
    forces, virial = pl.pallas_call(
        last_kernel,
        out_shape=(shape(3, 1, ATOMS), shape(3, 3)),
        compiler_params=params(),
        name="forces",
    )(closing, keep, local_grad, hot)
    return jnp.transpose(forces, (1, 0, 2)), site_energy, virial


def solution(mesh):
    by_domain = ("gx", "gy", "gz")
    placed = (
        P(by_domain, None, None),
        P(by_domain, None),
        P(by_domain, None),
        P(by_domain, None),
        P(by_domain, None),
        P(by_domain),
    ) + (P(),) * 7
    return jax.shard_map(
        body,
        mesh=mesh,
        in_specs=placed,
        out_specs=(P(by_domain, None, None), P(by_domain, None), P()),
        check_vma=False,
    )
```

```python
import math

import jax
import jax.numpy as jnp
import numpy as np
from jax import lax
from jax.experimental import pallas as pl
from jax.experimental.pallas import tpu as pltpu
from jax.sharding import PartitionSpec as P

CELLS = 6
LAYERS = 2
ATOMS = 72
EDGES = 1152
BLOCKS = 9
LANES = 128
MAIN = 64
COUNT = 8
F32 = jnp.float32
BF16 = jnp.bfloat16
HIGHEST = lax.Precision.HIGHEST
ROOT3 = math.sqrt(3.0)
RING = 28
STEPS = [(dx, dy) for dx in (-1, 0, 1) for dy in (-1, 0, 1) if (dx, dy) != (0, 0)]


RIM_SITES = (
    [(0, y) for y in range(6)]
    + [(5, y) for y in range(6)]
    + [(x, 0) for x in range(1, 5)]
    + [(x, 5) for x in range(1, 5)]
)


def ring_index(i, j):
    if i == 0:
        return j
    if i == 7:
        return 8 + j
    if j == 0:
        return 16 + i - 1
    return 22 + i - 1


def cell_number(i, j, k):
    if i in (0, 7) or j in (0, 7):
        return k * RING + ring_index(i, j)
    return 112 + k * 36 + (i - 1) * 6 + (j - 1)


SITE_RANGE = {1: [5], -1: [0], 0: list(range(6))}
CELL_RANGE = {1: [7], -1: [0], 0: list(range(1, 7))}


def face(ranges, dx, dy):
    return list(enumerate((a, b) for a in ranges[dx] for b in ranges[dy]))


def tables():
    send_sites = np.full((8, 4, 4, 8), -1, np.int32)
    send_cells = np.full((8, 4, 4, 8), -1, np.int32)
    source = np.full((256,), -1, np.int32)
    target = np.full((10 * LANES,), -1, np.int32)
    places = {0: 0, 3: 64, 1: LANES, 2: LANES + 64}
    landing = target[: 8 * LANES].reshape(8, 4, 4, 8)
    for n, (dx, dy) in enumerate(STEPS):
        for at, site in face(SITE_RANGE, dx, dy):
            for k in range(4):
                send_sites[n, :, k, at] = k * 32 + RIM_SITES.index(site)
        for at, (i, j) in face(CELL_RANGE, dx, dy):
            for k in range(4):
                send_cells[n, :3, k, at] = cell_number(i, j, k)
        for at, (x, y) in face(SITE_RANGE, -dx, -dy):
            i = {1: 7, -1: 0, 0: x + 1}[dx]
            j = {1: 7, -1: 0, 0: y + 1}[dy]
            for k in range(4):
                source[cell_number(i, j, k)] = n * LANES + k * 8 + at
        for at, (i, j) in face(CELL_RANGE, -dx, -dy):
            x = {1: 5, -1: 0, 0: i - 1}[dx]
            y = {1: 5, -1: 0, 0: j - 1}[dy]
            for k in range(4):
                landing[n, :3, k, at] = places[k] + x * 6 + y
    for x in range(CELLS):
        for y in range(CELLS):
            for k in range(4):
                own = cell_number(x + 1, y + 1, k)
                source[own] = 8 * LANES + places[k] + x * 6 + y
                target[8 * LANES + own] = places[k] + x * 6 + y
    row = np.arange(10 * LANES)[:, None]
    forward = np.where(row < 8 * LANES, row & ~96, row) == source
    back = target[:, None] == np.arange(256)
    lane = np.arange(LANES)[:, None]
    return forward, back, lane == send_sites.reshape(-1), lane == send_cells.reshape(-1)


TABLES = tables()


def parts_of(x, count):
    found = []
    for _ in range(count - 1):
        part = x.astype(BF16).astype(F32)
        found.append(part)
        x = x - part
    found.append(x)
    return found


def split_rows(x, count):
    return jnp.concatenate(parts_of(x, count), axis=0).astype(BF16)


def exact_dot(x, table, count=3):
    rows = x.shape[0]
    out = jnp.dot(split_rows(x, count), table, preferred_element_type=F32)
    return sum(out[i * rows : (i + 1) * rows] for i in range(1, count)) + out[:rows]


def exact_dot_nt(x, table, count=3):
    rows = x.shape[0]
    out = lax.dot_general(split_rows(x, count), table, (((1,), (1,)), ((), ())), preferred_element_type=F32)
    return sum(out[i * rows : (i + 1) * rows] for i in range(1, count)) + out[:rows]


def pad_rows(x):
    return jnp.concatenate([x, jnp.zeros((8 - x.shape[0], x.shape[1]), F32)], axis=0)


def iota(shape, dim):
    return lax.broadcasted_iota(jnp.int32, shape, dim)


def as_hot(mask):
    return jnp.where(mask, 1.0, 0.0).astype(BF16)


def start_fetch(sources, buffers, sems):
    copies = [pltpu.make_async_copy(src, dst, sems.at[n]) for n, (src, dst) in enumerate(zip(sources, buffers))]
    for copy in copies:
        copy.start()
    return copies


def fetch(sources, buffers, sems):
    for copy in start_fetch(sources, buffers, sems):
        copy.wait()


def atom_rows(pos_ref, kind_ref):
    kind = kind_ref[...].astype(F32)
    return jnp.concatenate([pos_ref[0], pos_ref[1], pos_ref[2], kind, jnp.zeros((4, ATOMS), F32)], axis=0)


def lane_sites():
    lane = iota((8, 3 * LANES), 1)
    part, at = lane >> 7, lane & 63
    second = (lane & 64) > 0
    rim = jnp.where(
        at < 12,
        jnp.where(at < 6, at, 24 + at),
        jnp.where(at < 16, 6 * (at - 11), 6 * (at - 15) + 5),
    )
    whole = jnp.where(at < 36, at, 1000)
    rim = jnp.where(at < 20, rim, 1000)
    layer = jnp.where(part == 0, jnp.where(second, 1, 0), part - 1)
    return 2 * jnp.where((part > 0) & second, rim, whole) + layer


def send_kernel(pos_hbm, kind_hbm, site_hbm, both_ref, down_ref, up_ref, hot_ref, pos_ref, kind_ref, site_ref, sems):
    fetch((pos_hbm, kind_hbm, site_hbm), (pos_ref, kind_ref, site_ref), sems)
    rows = atom_rows(pos_ref, kind_ref)
    hot = as_hot(iota((ATOMS, ATOMS), 0) == site_ref[...])
    pick = as_hot(iota((ATOMS, 3 * LANES), 0) == lane_sites()[0:1])
    placed = jnp.dot(hot, pick, preferred_element_type=F32).astype(BF16)
    out = exact_dot(rows, placed)
    both_ref[...] = out[:4, 0:LANES]
    down_ref[...] = out[:4, LANES : 2 * LANES]
    up_ref[...] = out[:4, 2 * LANES : 3 * LANES]
    hot_ref[...] = placed[:, 0:LANES]


def by_component(row):
    lane, comp = iota((8, LANES), 1), iota((8, LANES), 0)
    return jnp.where((lane >> 5) == comp, jnp.broadcast_to(row, (8, LANES)), 0.0)


def to_rows(x, table):
    out = exact_dot(x, table)
    keep = ((iota(out.shape, 1) >> 5) & 3) == iota(out.shape, 0)
    return jnp.sum(jnp.where(keep, out, 0.0), axis=0, keepdims=True)


def neighbour(n):
    dx, dy = STEPS[n]
    gx = lax.axis_index("gx")
    gy = lax.axis_index("gy")
    return lax.rem(gx + (dx + COUNT), COUNT) * COUNT + lax.rem(gy + (dy + COUNT), COUNT)


def column_kernel(down_ref, up_ref, below_ref, above_ref, table_ref, msg_ref, outer_ref):
    lane = iota((8, LANES), 1)

    def rim(x, at):
        return pltpu.roll(x, (at - 64) % LANES, 1)

    below, above, low, high = (pad_rows(ref[...]) for ref in (below_ref, above_ref, down_ref, up_ref))
    column = jnp.where(
        lane < 32,
        rim(below, 0),
        jnp.where(lane < 64, rim(low, 32), jnp.where(lane < 96, rim(high, 64), rim(above, 96))),
    )
    outer_ref[...] = jnp.where(lane < 64, below, pltpu.roll(above, 64, 1))[:4]
    rows = to_rows(column, table_ref[...])
    msg_ref[...] = jnp.zeros_like(msg_ref)
    for n in range(8):
        msg_ref[pl.ds(neighbour(n), 1), :] = rows[:, n * LANES : (n + 1) * LANES]


def cat_of(w):
    high = w.astype(BF16).astype(F32)
    low = w - high
    return jnp.concatenate([high, high, low], axis=1).astype(BF16)


def cell_shifts():
    lane = iota((8, 256), 1)
    row = iota((8, 256), 0)
    inside = lane - 112
    ring_layer = jnp.where(lane >= 28, 1, 0) + jnp.where(lane >= 56, 1, 0) + jnp.where(lane >= 84, 1, 0)
    ring = lane - 28 * ring_layer
    outer = lane < 112
    layer = jnp.where(
        outer,
        ring_layer,
        jnp.where(inside >= 36, 1, 0) + jnp.where(inside >= 72, 1, 0) + jnp.where(inside >= 108, 1, 0),
    )
    low_z = layer == 0
    high_z = layer == 3
    corner_low = (ring == 0) | (ring == 8)
    corner_high = (ring == 7) | (ring == 15)
    low_y = outer & (corner_low | ((ring >= 16) & (ring < 22)))
    high_y = outer & (corner_high | (ring >= 22))
    low_x = outer & (ring < 8)
    high_x = outer & (ring >= 8) & (ring < 16)

    def sides(low, high, edge):
        return jnp.where(high, edge, 0.0) - jnp.where(low, edge, 0.0)

    return jnp.where(
        row == 0,
        sides(low_x, high_x, 12.0),
        jnp.where(row == 1, sides(low_y, high_y, 12.0), jnp.where(row == 2, sides(low_z, high_z, 4.0), 0.0)),
    )


def prepare_kernel(count_ref, *refs):
    sources, outputs, buffers, sems = refs[:15], refs[15:30], refs[30:41], refs[41]
    copies = start_fetch(sources, buffers + outputs[11:], sems)
    make_slots(count_ref, copies[:4], buffers[:4], outputs[:4])
    make_weights(copies[4:11], buffers[4:], outputs[4:11])
    for copy in copies[11:]:
        copy.wait()


def make_slots(count_ref, copies, buffers, outputs):
    center_ref, other_ref, pos_ref, kind_ref = buffers
    cell_ref, live_ref, own_ref, shift_ref = outputs
    shift_ref[...] = cell_shifts()
    before = as_hot((iota((LANES, 256), 0) < iota((LANES, 256), 1)) | (iota((LANES, 256), 1) >= LANES))
    lane = iota((ATOMS, 256), 1)
    spread = as_hot(iota((ATOMS, 256), 0) == jnp.where(lane < LANES, lane & 63, MAIN + (lane & 7)))
    for copy in copies:
        copy.wait()
    center = center_ref[...]
    other = other_ref[...]
    atom = lax.broadcasted_iota(jnp.int32, (ATOMS, EDGES), 0)
    hot = jnp.where(atom == center, 1.0, 0.0)
    hot16 = hot.astype(BF16)
    running = jnp.zeros((ATOMS, LANES), F32)
    ranks = []
    for b in range(BLOCKS):
        at = slice(b * LANES, (b + 1) * LANES)
        sums = jnp.dot(hot16[:, at], before, preferred_element_type=F32)
        ranks.append(jnp.sum(hot[:, at] * (sums[:, :LANES] + running), axis=0, keepdims=True))
        running = running + sums[:, LANES:]
    rank = jnp.concatenate(ranks, axis=1).astype(jnp.int32)
    is_main = center < MAIN
    block = jnp.where(is_main, rank >> 1, BLOCKS - 1)
    lane = jnp.where(is_main, (rank & 1) * MAIN + center, rank * 8 + (center - MAIN))
    i, j, k = other >> 5, (other >> 2) & 7, other & 3
    ring = jnp.where(
        i == 0, j, jnp.where(i == 7, 8 + j, jnp.where(j == 0, 15 + i, jnp.where(j == 7, 21 + i, -1)))
    )
    cell = jnp.where(ring >= 0, k * RING + ring, 112 + k * 36 + (i - 1) * 6 + (j - 1)).astype(F32)
    slot = lax.broadcasted_iota(jnp.int32, (1, EDGES), 1)
    live = jnp.where(slot < count_ref[0], 1.0, 0.0)
    row = lax.broadcasted_iota(jnp.int32, (16, EDGES), 0)
    left = jnp.concatenate([jnp.where(row == block, cell, 0.0), jnp.where(row == block, live, 0.0)], axis=0)
    lane_hot = jnp.where(lax.broadcasted_iota(jnp.int32, (LANES, EDGES), 0) == lane, 1.0, 0.0).astype(BF16)
    placed = lax.dot_general(
        left.astype(BF16), lane_hot, (((1,), (1,)), ((), ())), preferred_element_type=F32
    )
    for b in range(BLOCKS):
        at = slice(b * LANES, (b + 1) * LANES)
        cell_ref[:, at] = placed[b : b + 1].astype(jnp.int32)
        live_ref[:, at] = placed[16 + b : 17 + b]
    own_ref[...] = exact_dot(atom_rows(pos_ref, kind_ref), spread)


def make_weights(copies, buffers, outputs):
    win_ref, w3_ref, wlat_ref, wlat_t_ref, w3_t_ref, win_t_ref, read_ref = outputs
    for copy in copies:
        copy.wait()
    w_in_ref, w_two_ref, w_env_ref, w_value_ref, w_latent_ref, w_out_ref, readout_ref = buffers
    w_in_t = w_in_ref[...]
    win_ref[...] = cat_of(w_in_t.T)
    w_two = w_two_ref[...]
    mixed = jnp.concatenate([w_env_ref[...], w_value_ref[...]], axis=0)
    w3 = jnp.concatenate(
        [w_two, jnp.dot(mixed, w_two, precision=HIGHEST, preferred_element_type=F32)], axis=0
    )
    w3_ref[...] = cat_of(w3)
    w3_t_ref[...] = cat_of(w3.T)
    w_latent = w_latent_ref[...]
    wlat_ref[...] = cat_of(w_latent)
    wlat_t_ref[...] = cat_of(w_latent.T)
    win_t_ref[...] = cat_of(w_in_t)
    square = lax.broadcasted_iota(jnp.int32, (64, 64), 0) == lax.broadcasted_iota(jnp.int32, (64, 64), 1)
    column = jnp.sum(jnp.where(square, readout_ref[...], 0.0), axis=1, keepdims=True)
    read_ref[...] = jnp.dot(
        w_out_ref[...].T,
        jnp.broadcast_to(column, (64, LANES)),
        precision=HIGHEST,
        preferred_element_type=F32,
    )


def cos_sin_pi(t):
    whole = jnp.floor(t + 0.5)
    f = t - whole
    half = whole * 0.5
    sign = 1.0 - 4.0 * (half - jnp.floor(half))
    a = f * math.pi
    q = a * a
    c = 1.0 + q * (
        -0.5
        + q * (1 / 24 + q * (-1 / 720 + q * (1 / 40320 + q * (-1 / 3628800 + q * (1 / 479001600)))))
    )
    s = a * (
        1.0
        + q
        * (-1 / 6 + q * (1 / 120 + q * (-1 / 5040 + q * (1 / 362880 + q * (-1 / 39916800 + q * (1 / 6227020800))))))
    )
    return c * sign, s * sign


def sum_slots(main, last):
    main = main + pltpu.roll(main, 64, 1)
    for shift in (64, 32, 16, 8):
        last = last + pltpu.roll(last, shift, 1)
    return main, last


def store_cat(ref, row, depth, at, x):
    high = x.astype(BF16)
    low = (x - high.astype(F32)).astype(BF16)
    ref[pl.ds(row, 16), at] = high
    ref[pl.ds(depth + row, 16), at] = low
    ref[pl.ds(2 * depth + row, 16), at] = high


def repeat(count, step):
    for n in range(count):
        step(n, 0)


def main_kernel(
    recv_ref,
    outer_ref,
    inner_ref,
    cell_ref,
    live_ref,
    own_ref,
    shift_ref,
    win_ref,
    w3_ref,
    wlat_ref,
    wlat_t_ref,
    w3_t_ref,
    win_t_ref,
    read_ref,
    forward_ref,
    cells_ref,
    msg_ref,
    ext_ref,
    local_ref,
    hot,
    harm,
    env_live,
    pre,
    slope,
    cat_a,
    cat_b,
    mixed,
    paths,
    environment,
    grad_lat,
    grad_harm,
    grad_env,
    energy,
):
    blocks = [slice(b * LANES, (b + 1) * LANES) for b in range(BLOCKS)]

    columns = [by_component(recv_ref[pl.ds(neighbour(n), 1), :]) for n in range(8)]
    columns += [pad_rows(outer_ref[...]), pad_rows(inner_ref[...])]
    arrived = jnp.concatenate(columns, axis=1)
    extended = exact_dot(arrived, forward_ref[...]) + shift_ref[...]
    cells = lax.broadcasted_iota(jnp.int32, (256, EDGES), 0)
    hot[...] = jnp.where(cells == cell_ref[...], 1.0, 0.0).astype(BF16)
    partner = exact_dot(extended, hot[...])
    own = own_ref[...]
    center = jnp.concatenate([own[:, :LANES]] * 8 + [own[:, LANES:]], axis=1)
    displacement = partner - center

    def wide(x, row):
        return jnp.broadcast_to(x[row : row + 1], (8, EDGES))

    x = wide(displacement, 0) * 0.2
    y = wide(displacement, 1) * 0.2
    z = wide(displacement, 2) * 0.2
    scaled = x * x + y * y + z * z
    live = jnp.broadcast_to(live_ref[...], (8, EDGES))
    env_live[...] = (1.0 - scaled) * (1.0 - scaled) * live
    harm[0] = x
    harm[1] = y
    harm[2] = z
    harm[3] = ROOT3 * x * y
    harm[4] = ROOT3 * y * z
    harm[5] = ROOT3 * x * z
    harm[6] = (0.5 * ROOT3) * (x * x - y * y)
    harm[7] = 0.5 * (2.0 * z * z - x * x - y * y)

    order = lax.broadcasted_iota(jnp.int32, (8, EDGES), 0)
    orders = order.astype(F32)
    radial, radial_sin = cos_sin_pi(orders * scaled)
    kinds = jnp.where(order < 4, wide(center, 3), wide(partner, 3) + 4.0)
    one_hot = jnp.where(kinds == orders, 1.0, 0.0)
    inputs = jnp.concatenate([radial, one_hot], axis=0)
    inputs_high = inputs.astype(BF16)
    inputs_low = (inputs - inputs_high.astype(F32)).astype(BF16)
    pre[0:16] = jnp.dot(
        win_ref[...],
        jnp.concatenate([inputs_high, inputs_low, inputs_high], axis=0),
        preferred_element_type=F32,
    ).reshape(16, 8, EDGES)

    def first_layer(c, carry):
        v = pre[pl.ds(2 * c, 2)]
        gate = 1.0 / (1.0 + jnp.exp(-v))
        out = v * gate
        slope[pl.ds(2 * c, 2)] = gate + out * (1.0 - gate)
        store_cat(cat_a, 16 * c, 128, slice(None), out.reshape(16, EDGES))
        return carry

    repeat(8, first_layer)
    mixed[...] = jnp.dot(w3_ref[...], cat_a[0:384], preferred_element_type=F32).reshape(24, 8, EDGES)

    def forward_tile(t, carry):
        sums = [[None, None] for _ in range(9)]
        for b, at in enumerate(blocks):
            weight = mixed[pl.ds(8 + 2 * t, 2), :, at] * env_live[:, at]
            part = 0 if b < 8 else 1
            for r in range(9):
                term = weight if r == 0 else weight * harm[r - 1, :, at]
                sums[r][part] = term if sums[r][part] is None else sums[r][part] + term
        found = []
        for r in range(9):
            main, last = sum_slots(sums[r][0].reshape(16, LANES), sums[r][1].reshape(16, LANES))
            main, last = main.reshape(2, 8, LANES), last.reshape(2, 8, LANES)
            environment[r, pl.ds(2 * t, 2), :, 0:LANES] = main
            environment[r, pl.ds(2 * t, 2), :, LANES : 2 * LANES] = last
            found.append((main, last))
        for b, at in enumerate(blocks):
            part = 0 if b < 8 else 1
            h = [None] + [harm[r, :, at] for r in range(8)]
            e = [found[r][part] for r in range(9)]
            one = h[1] * e[1] + h[2] * e[2] + h[3] * e[3]
            two = h[4] * e[4] + h[5] * e[5] + h[6] * e[6] + h[7] * e[7] + h[8] * e[8]
            paths[0, pl.ds(2 * t, 2), :, at] = one
            paths[1, pl.ds(2 * t, 2), :, at] = two
            values = mixed[pl.ds(16 + 2 * t, 2), :, at]
            base = 16 * t
            store_cat(cat_b, base, 256, at, mixed[pl.ds(2 * t, 2), :, at].reshape(16, LANES))
            store_cat(cat_b, 64 + base, 256, at, (e[0] * values).reshape(16, LANES))
            store_cat(cat_b, 128 + base, 256, at, (one * values).reshape(16, LANES))
            store_cat(cat_b, 192 + base, 256, at, (two * values).reshape(16, LANES))
        return carry

    repeat(4, forward_tile)
    pre[...] = jnp.dot(wlat_ref[...], cat_b[...], preferred_element_type=F32).reshape(16, 8, EDGES)
    energy[...] = jnp.zeros((8, EDGES), F32)

    def second_layer(c, carry):
        v = pre[pl.ds(2 * c, 2)]
        gate = 1.0 / (1.0 + jnp.exp(-v))
        out = v * gate
        weights = read_ref[pl.ds(16 * c, 16), :].reshape(2, 8, LANES)
        weights = jnp.concatenate([weights] * BLOCKS, axis=2)
        product = weights * out
        energy[...] += product[0] + product[1]
        back = weights * (gate + out * (1.0 - gate)) * env_live[...]
        store_cat(cat_a, 16 * c, 128, slice(None), back.reshape(16, EDGES))
        return carry

    repeat(8, second_layer)
    grad_lat[...] = jnp.dot(wlat_t_ref[...], cat_a[...], preferred_element_type=F32).reshape(32, 8, EDGES)
    grad_harm[...] = jnp.zeros((8, 8, EDGES), F32)
    grad_env[...] = jnp.zeros((8, EDGES), F32)

    def backward_tile(t, carry):
        base = 16 * t
        sums = [[None, None] for _ in range(9)]
        for b, at in enumerate(blocks):
            part = 0 if b < 8 else 1
            lanes = slice(part * LANES, (part + 1) * LANES)
            values = mixed[pl.ds(16 + 2 * t, 2), :, at]
            d = [grad_lat[pl.ds(8 + 8 * l + 2 * t, 2), :, at] for l in range(3)]
            zero = environment[0, pl.ds(2 * t, 2), :, lanes]
            one = paths[0, pl.ds(2 * t, 2), :, at]
            two = paths[1, pl.ds(2 * t, 2), :, at]
            d_values = d[0] * zero + d[1] * one + d[2] * two
            store_cat(cat_b, 128 + base, 192, at, d_values.reshape(16, LANES))
            store_cat(cat_b, base, 192, at, grad_lat[pl.ds(2 * t, 2), :, at].reshape(16, LANES))
            q = [d[l] * values for l in range(3)]
            for r in range(9):
                level = 0 if r == 0 else (1 if r < 4 else 2)
                term = q[0] if r == 0 else q[level] * harm[r - 1, :, at]
                sums[r][part] = term if sums[r][part] is None else sums[r][part] + term
        found = []
        for r in range(9):
            main, last = sum_slots(sums[r][0].reshape(16, LANES), sums[r][1].reshape(16, LANES))
            found.append((main.reshape(2, 8, LANES), last.reshape(2, 8, LANES)))
        for b, at in enumerate(blocks):
            part = 0 if b < 8 else 1
            lanes = slice(part * LANES, (part + 1) * LANES)
            raw = mixed[pl.ds(8 + 2 * t, 2), :, at]
            envelope = env_live[:, at]
            weight = raw * envelope
            values = mixed[pl.ds(16 + 2 * t, 2), :, at]
            q = [None] + [grad_lat[pl.ds(8 + 8 * l + 2 * t, 2), :, at] * values for l in (1, 2)]
            d_weight = found[0][part]
            for r in range(1, 9):
                g = found[r][part]
                d_weight = d_weight + harm[r - 1, :, at] * g
                level = 1 if r < 4 else 2
                term = q[level] * environment[r, pl.ds(2 * t, 2), :, lanes] + weight * g
                grad_harm[r - 1, :, at] += term[0] + term[1]
            slack = d_weight * raw
            grad_env[:, at] += slack[0] + slack[1]
            store_cat(cat_b, 64 + base, 192, at, (d_weight * envelope).reshape(16, LANES))
        return carry

    repeat(4, backward_tile)
    pre[...] = jnp.dot(w3_t_ref[...], cat_b[0:576], preferred_element_type=F32).reshape(16, 8, EDGES)

    def first_back(c, carry):
        back = pre[pl.ds(2 * c, 2)] * slope[pl.ds(2 * c, 2)]
        store_cat(cat_a, 16 * c, 128, slice(None), back.reshape(16, EDGES))
        return carry

    repeat(8, first_back)
    d_radial = jnp.dot(win_t_ref[...], cat_a[...], preferred_element_type=F32)[:8]

    x, y, z = harm[0], harm[1], harm[2]
    scaled = x * x + y * y + z * z
    live = jnp.broadcast_to(live_ref[...], (8, EDGES))
    d_scaled = d_radial * (orders * radial_sin) * (-math.pi) + (grad_env[...] + energy[...]) * (
        -2.0 * (1.0 - scaled) * live
    )
    g = [grad_harm[r] for r in range(8)]
    twice = 2.0 * d_scaled
    d_x = g[0] + ROOT3 * (y * g[3] + z * g[5] + x * g[6]) - x * g[7] + twice * x
    d_y = g[1] + ROOT3 * (x * g[3] + z * g[4] - y * g[6]) - y * g[7] + twice * y
    d_z = g[2] + ROOT3 * (y * g[4] + x * g[5]) + 2.0 * z * g[7] + twice * z
    e = energy[...] * env_live[...]
    rows = [jnp.sum(v, axis=0, keepdims=True) for v in (d_x * 0.2, d_y * 0.2, d_z * 0.2, e)]
    grads = jnp.concatenate(rows + [jnp.zeros((4, EDGES), F32)], axis=0)

    def over_blocks(v):
        total = v[:, blocks[0]]
        for b in range(1, 8):
            total = total + v[:, blocks[b]]
        return total

    main, last = sum_slots(over_blocks(grads), grads[:, blocks[8]])
    atoms = jnp.concatenate([main[:, :MAIN], last[:, : ATOMS - MAIN]], axis=1)
    local_ref[...] = atoms

    extended_grad = exact_dot_nt(grads, hot[...])
    ext_ref[...] = extended_grad[:4]
    lane = lax.broadcasted_iota(jnp.int32, (8, LANES), 1)
    row = lax.broadcasted_iota(jnp.int32, (8, LANES), 0)
    virial = jnp.zeros((8, LANES), F32)
    for a, comp in enumerate((x, y, z)):
        product = comp * grads
        total = jnp.sum(over_blocks(product) + product[:, blocks[8]], axis=1, keepdims=True)
        virial = jnp.where((lane == 96 + row + 3 * a) & (row < 3), total * 5.0, virial)
    virial = jnp.sum(virial, axis=0, keepdims=True)
    rows = to_rows(extended_grad[:, :LANES], cells_ref[...])
    msg_ref[...] = jnp.broadcast_to(virial, (COUNT * COUNT, LANES))
    for n in range(8):
        msg_ref[pl.ds(neighbour(n), 1), :] = rows[:, n * LANES : (n + 1) * LANES] + virial


def middle_kernel(recv_ref, ext_ref, back_ref, msg_ref, keep_ref):
    columns = [by_component(recv_ref[pl.ds(neighbour(n), 1), :]) for n in range(8)]
    arrived = jnp.concatenate(columns + [pad_rows(ext_ref[...])], axis=1)
    sums = exact_dot(arrived, back_ref[...])
    total = jnp.sum(recv_ref[...], axis=0, keepdims=True)
    message = jnp.concatenate([sums[:3, :LANES], total], axis=0)
    msg_ref[...] = jnp.broadcast_to(message[None], (COUNT, 4, LANES))
    keep_ref[...] = sums[:, LANES:]


def last_kernel(recv_ref, keep_ref, local_ref, hot_ref, force_ref, energy_ref, virial_ref):
    gz = lax.axis_index("gz")
    above = pad_rows(recv_ref[lax.rem(gz + 1, COUNT)])
    below = pad_rows(recv_ref[lax.rem(gz + (COUNT - 1), COUNT)])
    lane = lax.broadcasted_iota(jnp.int32, (8, LANES), 1)
    row = lax.broadcasted_iota(jnp.int32, (8, LANES), 0)
    sites = keep_ref[...] + jnp.where(lane < 64, pltpu.roll(below, 64, 1), pltpu.roll(above, 64, 1))
    atoms = exact_dot_nt(sites, hot_ref[...])
    energy_ref[...] = local_ref[3:4]
    force = local_ref[...] - atoms
    for comp in range(3):
        force_ref[comp] = force[comp : comp + 1]
    total = jnp.broadcast_to(jnp.sum(recv_ref[...], axis=0)[3:4], (8, LANES))
    normalizer = -1.0 / math.sqrt(EDGES * COUNT * COUNT * COUNT)
    virial = jnp.zeros((8, LANES), F32)
    for b in range(3):
        entry = jnp.sum(jnp.where(lane == 96 + 3 * row + b, total, 0.0), axis=1, keepdims=True)
        virial = jnp.where(lane == b, entry * normalizer, virial)
    virial_ref[...] = virial[:3, :3]


def shape(*dims, dtype=F32):
    return jax.ShapeDtypeStruct(dims, dtype)


def in_hbm(*arrays):
    return [pltpu.with_memory_space_constraint(x, pltpu.HBM) for x in arrays]


def fetched(arrays, more=0):
    return [pltpu.VMEM(x.shape, x.dtype) for x in arrays] + [pltpu.SemaphoreType.DMA((len(arrays) + more,))]


def params():
    return pltpu.CompilerParams(vmem_limit_bytes=48 * 1024 * 1024)


def body(
    positions,
    species,
    site_atom,
    edge_center,
    edge_other,
    edge_count,
    w_in,
    w_two,
    w_env,
    w_value,
    w_latent,
    w_out,
    readout,
):
    half = (4, LANES)
    hbm = pl.BlockSpec(memory_space=pltpu.HBM)
    columns_first = jnp.transpose(positions, (1, 0, 2))
    own, down, up, hot = pl.pallas_call(
        send_kernel,
        in_specs=[hbm] * 3,
        out_shape=(shape(*half), shape(*half), shape(*half), shape(ATOMS, LANES, dtype=BF16)),
        scratch_shapes=[
            pltpu.VMEM((3, 1, ATOMS), F32),
            pltpu.VMEM((1, ATOMS), jnp.int32),
            pltpu.VMEM((1, ATOMS), jnp.int32),
            pltpu.SemaphoreType.DMA((3,)),
        ],
        compiler_params=params(),
        name="sites",
    )(*in_hbm(columns_first, species, site_atom))
    ahead = [(i, (i + 1) % COUNT) for i in range(COUNT)]
    behind = [(target, source) for source, target in ahead]
    below = lax.ppermute(up, "gz", ahead)
    above = lax.ppermute(down, "gz", behind)

    inputs = (
        edge_center,
        edge_other,
        columns_first,
        species,
        w_in.T,
        w_two,
        w_env,
        w_value,
        w_latent,
        w_out,
        readout.reshape(1, 64),
    )
    routes = [jnp.asarray(table, BF16) for table in TABLES]
    prepared = pl.pallas_call(
        prepare_kernel,
        in_specs=[pl.BlockSpec(memory_space=pltpu.SMEM)] + [hbm] * (len(inputs) + 4),
        out_shape=(
            shape(1, EDGES, dtype=jnp.int32),
            shape(1, EDGES),
            shape(8, 256),
            shape(8, 256),
            shape(128, 48, dtype=BF16),
            shape(192, 384, dtype=BF16),
            shape(128, 768, dtype=BF16),
            shape(256, 384, dtype=BF16),
            shape(128, 576, dtype=BF16),
            shape(16, 384, dtype=BF16),
            shape(128, LANES),
            shape(10 * LANES, 256, dtype=BF16),
            shape(10 * LANES, 256, dtype=BF16),
            shape(LANES, 8 * LANES, dtype=BF16),
            shape(LANES, 8 * LANES, dtype=BF16),
        ),
        scratch_shapes=fetched(inputs, 4),
        compiler_params=params(),
        cost_estimate=pl.CostEstimate(flops=10_000_000, bytes_accessed=2_000_000, transcendentals=0),
        name="slots_and_weights",
    )(edge_count, *in_hbm(*inputs, *routes))

    planes = (COUNT * COUNT, LANES)
    column, outer = pl.pallas_call(
        column_kernel,
        out_shape=(shape(*planes), shape(*half)),
        compiler_params=params(),
        name="column",
    )(down, up, below, above, prepared[13])
    arrived = lax.all_to_all(column, ("gx", "gy"), 0, 0)

    message, extended_grad, local_grad = pl.pallas_call(
        main_kernel,
        out_shape=(shape(*planes), shape(4, 256), shape(8, ATOMS)),
        scratch_shapes=[
            pltpu.VMEM((256, EDGES), BF16),
            pltpu.VMEM((8, 8, EDGES), F32),
            pltpu.VMEM((8, EDGES), F32),
            pltpu.VMEM((16, 8, EDGES), F32),
            pltpu.VMEM((16, 8, EDGES), F32),
            pltpu.VMEM((384, EDGES), BF16),
            pltpu.VMEM((768, EDGES), BF16),
            pltpu.VMEM((24, 8, EDGES), F32),
            pltpu.VMEM((2, 8, 8, EDGES), F32),
            pltpu.VMEM((9, 8, 8, 256), F32),
            pltpu.VMEM((32, 8, EDGES), F32),
            pltpu.VMEM((8, 8, EDGES), F32),
            pltpu.VMEM((8, EDGES), F32),
            pltpu.VMEM((8, EDGES), F32),
        ],
        compiler_params=params(),
        name="edges",
    )(arrived, outer, own, *prepared[:12], prepared[14])
    returned = lax.all_to_all(message, ("gx", "gy"), 0, 0)
    layers, keep = pl.pallas_call(
        middle_kernel,
        out_shape=(shape(COUNT, 4, LANES), shape(8, LANES)),
        compiler_params=params(),
        name="columns_back",
    )(returned, extended_grad, prepared[12])
    closing = lax.all_to_all(layers, "gz", 0, 0)
    forces, site_energy, virial = pl.pallas_call(
        last_kernel,
        out_shape=(shape(3, 1, ATOMS), shape(1, ATOMS), shape(3, 3)),
        compiler_params=params(),
        name="forces",
    )(closing, keep, local_grad, hot)
    return jnp.transpose(forces, (1, 0, 2)), site_energy, virial


def solution(mesh):
    by_domain = ("gx", "gy", "gz")
    placed = (
        P(by_domain, None, None),
        P(by_domain, None),
        P(by_domain, None),
        P(by_domain, None),
        P(by_domain, None),
        P(by_domain),
    ) + (P(),) * 7
    return jax.shard_map(
        body,
        mesh=mesh,
        in_specs=placed,
        out_specs=(P(by_domain, None, None), P(by_domain, None), P()),
        check_vma=False,
    )
```

```python
import math

import jax
import jax.numpy as jnp
import numpy as np
from jax import lax
from jax.experimental import pallas as pl
from jax.experimental.pallas import tpu as pltpu
from jax.sharding import PartitionSpec as P

CELLS = 6
LAYERS = 2
ATOMS = 72
EDGES = 1152
BLOCKS = 9
LANES = 128
MAIN = 64
COUNT = 8
F32 = jnp.float32
BF16 = jnp.bfloat16
HIGHEST = lax.Precision.HIGHEST
ROOT3 = math.sqrt(3.0)
RING = 28
STEPS = [(dx, dy) for dx in (-1, 0, 1) for dy in (-1, 0, 1) if (dx, dy) != (0, 0)]


SITE_RANGE = {1: [5], -1: [0], 0: list(range(6))}
def face(dx, dy):
    return list(enumerate((x, y) for x in SITE_RANGE[dx] for y in SITE_RANGE[dy]))


def tables():
    routes = np.zeros((512, 256), np.float32)
    layers = {0: 0, 3: 64, 1: LANES, 2: LANES + 64}
    for k in range(4):
        for n, (dx, dy) in enumerate(STEPS):
            for m, (x, y) in face(dx, dy):
                place, column = n * 32 + k * 8 + m, layers[k] + x * 6 + y
                routes[column, place] = 1.0
                routes[256 + place, column] = 1.0
    return routes


ROUTES = tables()


def parts_of(x, count):
    found = []
    for _ in range(count - 1):
        part = x.astype(BF16).astype(F32)
        found.append(part)
        x = x - part
    found.append(x)
    return found


def split_rows(x, count):
    return jnp.concatenate(parts_of(x, count), axis=0).astype(BF16)


def exact_dot(x, table, count=3):
    rows = x.shape[0]
    out = jnp.dot(split_rows(x, count), table, preferred_element_type=F32)
    return sum(out[i * rows : (i + 1) * rows] for i in range(1, count)) + out[:rows]


def exact_dot_nt(x, table, count=3):
    rows = x.shape[0]
    out = lax.dot_general(split_rows(x, count), table, (((1,), (1,)), ((), ())), preferred_element_type=F32)
    return sum(out[i * rows : (i + 1) * rows] for i in range(1, count)) + out[:rows]


def pad_rows(x):
    return jnp.concatenate([x, jnp.zeros((8 - x.shape[0], x.shape[1]), F32)], axis=0)


def iota(shape, dim):
    return lax.broadcasted_iota(jnp.int32, shape, dim)


def as_hot(mask):
    return jnp.where(mask, 1.0, 0.0).astype(BF16)


def start_fetch(sources, buffers, sems):
    copies = [pltpu.make_async_copy(src, dst, sems.at[n]) for n, (src, dst) in enumerate(zip(sources, buffers))]
    for copy in copies:
        copy.start()
    return copies


def atom_rows(pos_ref, kind_ref):
    kind = kind_ref[...].astype(F32)
    return jnp.concatenate([pos_ref[0], pos_ref[1], pos_ref[2], kind, jnp.zeros((4, ATOMS), F32)], axis=0)


def lane_sites():
    lane = iota((8, LANES), 1)
    at = lane & 63
    return jnp.where(at < 36, 2 * at + (lane >> 6), -1)


def low_half(x, y):
    return jnp.where(iota(x.shape, 1) < 64, x, y)


def even_layer():
    return (lax.axis_index("gz") & 1) == 0


def send_kernel(*refs):
    sources, (both_ref, first_ref, second_ref, hot_ref), copied = refs[:13], refs[13:17], refs[17:29]
    pos_ref, kind_ref, site_ref = copied[0], copied[1], refs[29]
    copies = start_fetch(sources, (site_ref,) + copied, refs[30])
    for copy in copies[:3]:
        copy.wait()
    rows = atom_rows(pos_ref, kind_ref)
    hot = as_hot(iota((ATOMS, ATOMS), 0) == site_ref[...])
    pick = as_hot(iota((ATOMS, LANES), 0) == lane_sites()[0:1])
    placed = jnp.dot(hot, pick, preferred_element_type=F32).astype(BF16)
    both = exact_dot(rows, placed)
    turned = pltpu.roll(both, 64, 1)
    down = [low_half(both[c : c + 1], turned[c + 1 : c + 2]) for c in (0, 2)]
    up = [low_half(turned[c : c + 1], both[c + 1 : c + 2]) for c in (0, 2)]
    for c in range(2):
        first_ref[c : c + 1] = jnp.where(even_layer(), down[c], up[c])
        second_ref[c : c + 1] = jnp.where(even_layer(), up[c], down[c])
    both_ref[...] = both[:4]
    hot_ref[...] = placed
    for copy in copies[3:]:
        copy.wait()


def on_component():
    return (iota((8, LANES), 1) >> 5) == iota((8, LANES), 0)


def turn(x, step):
    comp = iota((8, LANES), 0)
    out = x
    for c in range(1, 4):
        out = jnp.where(comp == c, pltpu.roll(x, c * step % LANES, 1), out)
    return out


def from_rows(rows):
    halves = []
    for h in range(2):
        total = jnp.zeros((8, LANES), F32)
        for m in range(4):
            part = jnp.where(on_component(), jnp.broadcast_to(rows[4 * h + m], (8, LANES)), 0.0)
            total = total + (pltpu.roll(part, 32 * m, 1) if m else part)
        halves.append(turn(total, -32))
    return halves


def to_rows(x):
    rows = []
    for h in range(2):
        turned = turn(x[:, h * LANES : (h + 1) * LANES], 32)
        for m in range(4):
            part = pltpu.roll(turned, LANES - 32 * m, 1) if m else turned
            rows.append(jnp.sum(jnp.where(on_component(), part, 0.0), axis=0, keepdims=True))
    return rows


def neighbour(n):
    dx, dy = STEPS[n]
    gx = lax.axis_index("gx")
    gy = lax.axis_index("gy")
    return lax.rem(gx + (dx + COUNT), COUNT) * COUNT + lax.rem(gy + (dy + COUNT), COUNT)


def column_kernel(inner_ref, first_ref, second_ref, routes_ref, tie_ref, msg_ref, outer_ref):
    first, second = first_ref[...], second_ref[...]
    below = jnp.where(even_layer(), first, second)
    above = jnp.where(even_layer(), second, first)
    below_turned, above_turned = pltpu.roll(below, 64, 1), pltpu.roll(above, 64, 1)
    rows = []
    for c in range(2):
        at = slice(c, c + 1)
        rows += [low_half(below[at], above_turned[at]), low_half(below_turned[at], above[at])]
    outer = pad_rows(jnp.concatenate(rows, axis=0))
    outer_ref[...] = outer[:4]
    column = jnp.concatenate([outer, pad_rows(inner_ref[...])], axis=1)
    rows = to_rows(exact_dot(column, routes_ref[:256]))
    msg_ref[...] = jnp.zeros_like(msg_ref)
    for n in range(8):
        msg_ref[pl.ds(neighbour(n), 1), :] = rows[n]


def cat_of(w):
    high = w.astype(BF16).astype(F32)
    low = w - high
    both = jnp.concatenate([high, low], axis=0)
    return jnp.concatenate([both, both], axis=1).astype(BF16)


def dot_cat(w, x):
    out = jnp.dot(w, x, preferred_element_type=F32)
    rows = out.shape[0] // 2
    return out[:rows] + out[rows:]


def cell_shifts():
    lane = iota((8, 512), 1)
    row = iota((8, 512), 0)
    outer = lane < 256
    code = lane >> 5
    code = code + jnp.where(code >= 4, 1, 0)
    third = jnp.where(code >= 3, 1, 0) + jnp.where(code >= 6, 1, 0)
    along_x = jnp.where(outer, third - 1, 0)
    along_y = jnp.where(outer, code - 3 * third - 1, 0)
    layer = (lane >> 3) & 3
    part = lane >> 6
    low_z = jnp.where(outer, layer, part - 4) == 0
    high_z = jnp.where(outer, layer, part - 2) == 3
    along_z = jnp.where(high_z, 1, 0) - jnp.where(low_z, 1, 0)
    shift = jnp.where(row == 0, 12 * along_x, jnp.where(row == 1, 12 * along_y, 4 * along_z))
    return jnp.where(row < 3, shift, 0).astype(F32)


def prepare_kernel(count_ref, *refs):
    inputs, outputs = refs[:11], refs[11:]
    make_slots(count_ref, inputs[:4], outputs[:4])
    make_weights(inputs[4:], outputs[4:])


def make_slots(count_ref, buffers, outputs):
    pos_ref, kind_ref, center_ref, other_ref = buffers
    cell_ref, live_ref, own_ref, shift_ref = outputs
    shift_ref[...] = cell_shifts()
    before = as_hot((iota((LANES, 256), 0) < iota((LANES, 256), 1)) | (iota((LANES, 256), 1) >= LANES))
    lane = iota((ATOMS, 256), 1)
    spread = as_hot(iota((ATOMS, 256), 0) == jnp.where(lane < LANES, lane & 63, MAIN + (lane & 7)))
    center = center_ref[...]
    other = other_ref[...]
    atom = lax.broadcasted_iota(jnp.int32, (ATOMS, EDGES), 0)
    hot = jnp.where(atom == center, 1.0, 0.0)
    hot16 = hot.astype(BF16)
    running = jnp.zeros((ATOMS, LANES), F32)
    ranks = []
    for b in range(BLOCKS):
        at = slice(b * LANES, (b + 1) * LANES)
        sums = jnp.dot(hot16[:, at], before, preferred_element_type=F32)
        ranks.append(jnp.sum(hot[:, at] * (sums[:, :LANES] + running), axis=0, keepdims=True))
        running = running + sums[:, LANES:]
    rank = jnp.concatenate(ranks, axis=1).astype(jnp.int32)
    is_main = center < MAIN
    block = jnp.where(is_main, rank >> 1, BLOCKS - 1)
    lane = jnp.where(is_main, (rank & 1) * MAIN + center, rank * 8 + (center - MAIN))
    i, j, k = other >> 5, (other >> 2) & 7, other & 3
    dx = jnp.where(i == 7, 1, 0) - jnp.where(i == 0, 1, 0)
    dy = jnp.where(j == 7, 1, 0) - jnp.where(j == 0, 1, 0)
    code = 3 * dx + dy + 4
    place = jnp.where(dx == 0, i - 1, 0) + jnp.where(dy == 0, j - 1, 0)
    layer = jnp.where(k == 3, 64, jnp.where(k > 0, 64 * k + 64, 0))
    cell = jnp.where(
        code == 4,
        256 + layer + (i - 1) * 6 + (j - 1),
        (code - jnp.where(code > 4, 1, 0)) * 32 + k * 8 + place,
    )
    slot = lax.broadcasted_iota(jnp.int32, (1, EDGES), 1)
    live = jnp.where(slot < count_ref[0], 1.0, 0.0)
    row = lax.broadcasted_iota(jnp.int32, (16, EDGES), 0)
    values = ((cell & 255).astype(F32), (cell >> 8).astype(F32), live)
    left = jnp.concatenate([jnp.where(row == block, v, 0.0) for v in values], axis=0)
    lane_hot = jnp.where(lax.broadcasted_iota(jnp.int32, (LANES, EDGES), 0) == lane, 1.0, 0.0).astype(BF16)
    placed = lax.dot_general(
        left.astype(BF16), lane_hot, (((1,), (1,)), ((), ())), preferred_element_type=F32
    )
    for b in range(BLOCKS):
        at = slice(b * LANES, (b + 1) * LANES)
        cell_ref[:, at] = (placed[b : b + 1] + 256.0 * placed[16 + b : 17 + b]).astype(jnp.int32)
        live_ref[:, at] = placed[32 + b : 33 + b]
    own_ref[...] = exact_dot(atom_rows(pos_ref, kind_ref), spread)


def make_weights(buffers, outputs):
    win_ref, w3_ref, wlat_ref, wlat_t_ref, w3_t_ref, win_t_ref, read_ref = outputs
    w_in_ref, w_two_ref, w_env_ref, w_value_ref, w_latent_ref, w_out_ref, readout_ref = buffers
    w_in_t = w_in_ref[...]
    win_ref[...] = cat_of(w_in_t.T)
    w_two = w_two_ref[...]
    mixed = jnp.concatenate([w_env_ref[...], w_value_ref[...]], axis=0)
    w3 = jnp.concatenate(
        [w_two, jnp.dot(mixed, w_two, precision=HIGHEST, preferred_element_type=F32)], axis=0
    )
    w3_ref[...] = cat_of(w3)
    w3_t_ref[...] = cat_of(w3.T)
    w_latent = w_latent_ref[...]
    wlat_ref[...] = cat_of(w_latent)
    wlat_t_ref[...] = cat_of(w_latent.T)
    win_t_ref[...] = cat_of(w_in_t)
    square = lax.broadcasted_iota(jnp.int32, (64, 64), 0) == lax.broadcasted_iota(jnp.int32, (64, 64), 1)
    column = jnp.sum(jnp.where(square, readout_ref[...], 0.0), axis=1, keepdims=True)
    read_ref[...] = jnp.dot(
        w_out_ref[...].T,
        jnp.broadcast_to(column, (64, LANES)),
        precision=HIGHEST,
        preferred_element_type=F32,
    )


def cos_sin_pi(t):
    whole = jnp.floor(t + 0.5)
    f = t - whole
    half = whole * 0.5
    sign = 1.0 - 4.0 * (half - jnp.floor(half))
    a = f * math.pi
    q = a * a
    c = 1.0 + q * (
        -0.5
        + q * (1 / 24 + q * (-1 / 720 + q * (1 / 40320 + q * (-1 / 3628800 + q * (1 / 479001600)))))
    )
    s = a * (
        1.0
        + q
        * (-1 / 6 + q * (1 / 120 + q * (-1 / 5040 + q * (1 / 362880 + q * (-1 / 39916800 + q * (1 / 6227020800))))))
    )
    return c * sign, s * sign


def sum_slots(main, last):
    main = main + pltpu.roll(main, 64, 1)
    for shift in (64, 32, 16, 8):
        last = last + pltpu.roll(last, shift, 1)
    return main, last


def store_cat(ref, row, depth, at, x):
    high = x.astype(BF16)
    low = (x - high.astype(F32)).astype(BF16)
    ref[pl.ds(row, 16), at] = high
    ref[pl.ds(depth + row, 16), at] = low


def repeat(count, step):
    for n in range(count):
        step(n, 0)


def main_kernel(
    recv_ref,
    outer_ref,
    inner_ref,
    cell_ref,
    live_ref,
    own_ref,
    shift_ref,
    win_ref,
    w3_ref,
    wlat_ref,
    wlat_t_ref,
    w3_t_ref,
    win_t_ref,
    read_ref,
    msg_ref,
    ext_ref,
    local_ref,
    hot,
    harm,
    env_live,
    pre,
    slope,
    cat_a,
    cat_b,
    mixed,
    paths,
    environment,
    grad_lat,
    grad_harm,
    grad_env,
    energy,
):
    blocks = [slice(b * LANES, (b + 1) * LANES) for b in range(BLOCKS)]

    columns = from_rows([recv_ref[pl.ds(neighbour(n), 1), :] for n in range(8)])
    columns += [pad_rows(outer_ref[...]), pad_rows(inner_ref[...])]
    extended = jnp.concatenate(columns, axis=1) + shift_ref[...]
    cells = lax.broadcasted_iota(jnp.int32, (512, EDGES), 0)
    hot[...] = jnp.where(cells == cell_ref[...], 1.0, 0.0).astype(BF16)
    partner = exact_dot(extended, hot[...])
    own = own_ref[...]
    center = jnp.concatenate([own[:, :LANES]] * 8 + [own[:, LANES:]], axis=1)
    displacement = partner - center

    def wide(x, row):
        return jnp.broadcast_to(x[row : row + 1], (8, EDGES))

    x = wide(displacement, 0) * 0.2
    y = wide(displacement, 1) * 0.2
    z = wide(displacement, 2) * 0.2
    scaled = x * x + y * y + z * z
    live = jnp.broadcast_to(live_ref[...], (8, EDGES))
    env_live[...] = (1.0 - scaled) * (1.0 - scaled) * live
    harm[0] = x
    harm[1] = y
    harm[2] = z
    harm[3] = ROOT3 * x * y
    harm[4] = ROOT3 * y * z
    harm[5] = ROOT3 * x * z
    harm[6] = (0.5 * ROOT3) * (x * x - y * y)
    harm[7] = 0.5 * (2.0 * z * z - x * x - y * y)

    order = lax.broadcasted_iota(jnp.int32, (8, EDGES), 0)
    orders = order.astype(F32)
    radial, radial_sin = cos_sin_pi(orders * scaled)
    kinds = jnp.where(order < 4, wide(center, 3), wide(partner, 3) + 4.0)
    one_hot = jnp.where(kinds == orders, 1.0, 0.0)
    inputs = jnp.concatenate([radial, one_hot], axis=0)
    inputs_high = inputs.astype(BF16)
    inputs_low = (inputs - inputs_high.astype(F32)).astype(BF16)
    pre[...] = dot_cat(win_ref[...], jnp.concatenate([inputs_high, inputs_low], axis=0)).reshape(16, 8, EDGES)

    def first_layer(c, carry):
        v = pre[pl.ds(2 * c, 2)]
        gate = 1.0 / (1.0 + jnp.exp(-v))
        out = v * gate
        slope[pl.ds(2 * c, 2)] = gate + out * (1.0 - gate)
        store_cat(cat_a, 16 * c, 128, slice(None), out.reshape(16, EDGES))
        return carry

    repeat(8, first_layer)
    mixed[...] = dot_cat(w3_ref[...], cat_a[...]).reshape(24, 8, EDGES)

    def forward_tile(t, carry):
        sums = [[None, None] for _ in range(9)]
        for b, at in enumerate(blocks):
            weight = mixed[pl.ds(8 + 2 * t, 2), :, at] * env_live[:, at]
            part = 0 if b < 8 else 1
            for r in range(9):
                term = weight if r == 0 else weight * harm[r - 1, :, at]
                sums[r][part] = term if sums[r][part] is None else sums[r][part] + term
        found = []
        for r in range(9):
            main, last = sum_slots(sums[r][0].reshape(16, LANES), sums[r][1].reshape(16, LANES))
            main, last = main.reshape(2, 8, LANES), last.reshape(2, 8, LANES)
            environment[r, pl.ds(2 * t, 2), :, 0:LANES] = main
            environment[r, pl.ds(2 * t, 2), :, LANES : 2 * LANES] = last
            found.append((main, last))
        for b, at in enumerate(blocks):
            part = 0 if b < 8 else 1
            h = [None] + [harm[r, :, at] for r in range(8)]
            e = [found[r][part] for r in range(9)]
            one = h[1] * e[1] + h[2] * e[2] + h[3] * e[3]
            two = h[4] * e[4] + h[5] * e[5] + h[6] * e[6] + h[7] * e[7] + h[8] * e[8]
            paths[0, pl.ds(2 * t, 2), :, at] = one
            paths[1, pl.ds(2 * t, 2), :, at] = two
            values = mixed[pl.ds(16 + 2 * t, 2), :, at]
            base = 16 * t
            store_cat(cat_b, base, 256, at, mixed[pl.ds(2 * t, 2), :, at].reshape(16, LANES))
            store_cat(cat_b, 64 + base, 256, at, (e[0] * values).reshape(16, LANES))
            store_cat(cat_b, 128 + base, 256, at, (one * values).reshape(16, LANES))
            store_cat(cat_b, 192 + base, 256, at, (two * values).reshape(16, LANES))
        return carry

    repeat(4, forward_tile)
    pre[...] = dot_cat(wlat_ref[...], cat_b[...]).reshape(16, 8, EDGES)
    energy[...] = jnp.zeros((8, EDGES), F32)

    def second_layer(c, carry):
        v = pre[pl.ds(2 * c, 2)]
        gate = 1.0 / (1.0 + jnp.exp(-v))
        out = v * gate
        weights = read_ref[pl.ds(16 * c, 16), :].reshape(2, 8, LANES)
        weights = jnp.concatenate([weights] * BLOCKS, axis=2)
        product = weights * out
        energy[...] += product[0] + product[1]
        back = weights * (gate + out * (1.0 - gate)) * env_live[...]
        store_cat(cat_a, 16 * c, 128, slice(None), back.reshape(16, EDGES))
        return carry

    repeat(8, second_layer)
    grad_lat[...] = dot_cat(wlat_t_ref[...], cat_a[...]).reshape(32, 8, EDGES)
    grad_harm[...] = jnp.zeros((8, 8, EDGES), F32)
    grad_env[...] = jnp.zeros((8, EDGES), F32)

    def backward_tile(t, carry):
        base = 16 * t
        sums = [[None, None] for _ in range(9)]
        for b, at in enumerate(blocks):
            part = 0 if b < 8 else 1
            lanes = slice(part * LANES, (part + 1) * LANES)
            values = mixed[pl.ds(16 + 2 * t, 2), :, at]
            d = [grad_lat[pl.ds(8 + 8 * l + 2 * t, 2), :, at] for l in range(3)]
            zero = environment[0, pl.ds(2 * t, 2), :, lanes]
            one = paths[0, pl.ds(2 * t, 2), :, at]
            two = paths[1, pl.ds(2 * t, 2), :, at]
            d_values = d[0] * zero + d[1] * one + d[2] * two
            store_cat(cat_b, 128 + base, 192, at, d_values.reshape(16, LANES))
            store_cat(cat_b, base, 192, at, grad_lat[pl.ds(2 * t, 2), :, at].reshape(16, LANES))
            q = [d[l] * values for l in range(3)]
            for r in range(9):
                level = 0 if r == 0 else (1 if r < 4 else 2)
                term = q[0] if r == 0 else q[level] * harm[r - 1, :, at]
                sums[r][part] = term if sums[r][part] is None else sums[r][part] + term
        found = []
        for r in range(9):
            main, last = sum_slots(sums[r][0].reshape(16, LANES), sums[r][1].reshape(16, LANES))
            found.append((main.reshape(2, 8, LANES), last.reshape(2, 8, LANES)))
        for b, at in enumerate(blocks):
            part = 0 if b < 8 else 1
            lanes = slice(part * LANES, (part + 1) * LANES)
            raw = mixed[pl.ds(8 + 2 * t, 2), :, at]
            envelope = env_live[:, at]
            weight = raw * envelope
            values = mixed[pl.ds(16 + 2 * t, 2), :, at]
            q = [None] + [grad_lat[pl.ds(8 + 8 * l + 2 * t, 2), :, at] * values for l in (1, 2)]
            d_weight = found[0][part]
            for r in range(1, 9):
                g = found[r][part]
                d_weight = d_weight + harm[r - 1, :, at] * g
                level = 1 if r < 4 else 2
                term = q[level] * environment[r, pl.ds(2 * t, 2), :, lanes] + weight * g
                grad_harm[r - 1, :, at] += term[0] + term[1]
            slack = d_weight * raw
            grad_env[:, at] += slack[0] + slack[1]
            store_cat(cat_b, 64 + base, 192, at, (d_weight * envelope).reshape(16, LANES))
        return carry

    repeat(4, backward_tile)
    pre[...] = dot_cat(w3_t_ref[...], cat_b[0:384]).reshape(16, 8, EDGES)

    def first_back(c, carry):
        back = pre[pl.ds(2 * c, 2)] * slope[pl.ds(2 * c, 2)]
        store_cat(cat_a, 16 * c, 128, slice(None), back.reshape(16, EDGES))
        return carry

    repeat(8, first_back)
    d_radial = dot_cat(win_t_ref[...], cat_a[...])[:8]

    x, y, z = harm[0], harm[1], harm[2]
    scaled = x * x + y * y + z * z
    live = jnp.broadcast_to(live_ref[...], (8, EDGES))
    d_scaled = d_radial * (orders * radial_sin) * (-math.pi) + (grad_env[...] + energy[...]) * (
        -2.0 * (1.0 - scaled) * live
    )
    g = [grad_harm[r] for r in range(8)]
    twice = 2.0 * d_scaled
    d_x = g[0] + ROOT3 * (y * g[3] + z * g[5] + x * g[6]) - x * g[7] + twice * x
    d_y = g[1] + ROOT3 * (x * g[3] + z * g[4] - y * g[6]) - y * g[7] + twice * y
    d_z = g[2] + ROOT3 * (y * g[4] + x * g[5]) + 2.0 * z * g[7] + twice * z
    e = energy[...] * env_live[...]
    partial = [d_x * 0.2, d_y * 0.2, d_z * 0.2]
    extended_grad = exact_dot_nt(jnp.concatenate(partial, axis=0), hot[...], 2)

    def over_blocks(v):
        total = v[:, blocks[0]]
        for b in range(1, 8):
            total = total + v[:, blocks[b]]
        return total

    def summed(arrays):
        rows = [jnp.sum(v, axis=0, keepdims=True) for v in arrays]
        return jnp.concatenate(rows + [jnp.zeros((8 - len(rows), rows[0].shape[1]), F32)], axis=0)

    virial = []
    for a, comp in enumerate((x, y, z)):
        for b in range(3):
            product = comp * partial[b]
            virial.append(over_blocks(product) + product[:, blocks[8]])
    totals = jnp.sum(jnp.concatenate(virial, axis=0), axis=1, keepdims=True)
    lane = lax.broadcasted_iota(jnp.int32, (8, LANES), 1)
    virial = jnp.zeros((8, LANES), F32)
    for n in range(9):
        virial = jnp.where(lane == 96 + n, totals[8 * n : 8 * n + 8] * 5.0, virial)
    virial = jnp.sum(virial, axis=0, keepdims=True)

    extended_grad = summed([extended_grad[8 * c : 8 * c + 8] for c in range(3)])
    rows = to_rows(extended_grad[:, :256])
    msg_ref[...] = jnp.broadcast_to(virial, (COUNT * COUNT, LANES))
    for n in range(8):
        msg_ref[pl.ds(neighbour(n), 1), :] = rows[n] + virial
    ext_ref[...] = extended_grad[:4, 256:]

    arrays = partial + [e]
    main, last = sum_slots(summed([over_blocks(v) for v in arrays]), summed([v[:, blocks[8]] for v in arrays]))
    local_ref[...] = jnp.concatenate([main[:, :MAIN], last[:, : ATOMS - MAIN]], axis=1)


def middle_kernel(recv_ref, ext_ref, routes_ref, msg_ref, keep_ref):
    columns = from_rows([recv_ref[pl.ds(neighbour(n), 1), :] for n in range(8)])
    sums = exact_dot(jnp.concatenate(columns, axis=1), routes_ref[256:], 2) + pad_rows(ext_ref[...])
    total = jnp.sum(recv_ref[...], axis=0, keepdims=True)
    message = jnp.concatenate([sums[:3, :LANES], total], axis=0)
    msg_ref[...] = jnp.broadcast_to(message[None], (COUNT, 4, LANES))
    keep_ref[...] = sums[:, LANES:]


def last_kernel(recv_ref, keep_ref, local_ref, hot_ref, force_ref, energy_ref, virial_ref):
    gz = lax.axis_index("gz")
    above = pad_rows(recv_ref[lax.rem(gz + 1, COUNT)])
    below = pad_rows(recv_ref[lax.rem(gz + (COUNT - 1), COUNT)])
    lane = lax.broadcasted_iota(jnp.int32, (8, LANES), 1)
    row = lax.broadcasted_iota(jnp.int32, (8, LANES), 0)
    sites = keep_ref[...] + jnp.where(lane < 64, pltpu.roll(below, 64, 1), pltpu.roll(above, 64, 1))
    atoms = exact_dot_nt(sites, hot_ref[...], 2)
    energy_ref[...] = local_ref[3:4]
    force = local_ref[...] - atoms
    for comp in range(3):
        force_ref[comp] = force[comp : comp + 1]
    total = jnp.broadcast_to(jnp.sum(recv_ref[...], axis=0)[3:4], (8, LANES))
    normalizer = -1.0 / math.sqrt(EDGES * COUNT * COUNT * COUNT)
    virial = jnp.zeros((8, LANES), F32)
    for b in range(3):
        entry = jnp.sum(jnp.where(lane == 96 + 3 * row + b, total, 0.0), axis=1, keepdims=True)
        virial = jnp.where(lane == b, entry * normalizer, virial)
    virial_ref[...] = virial[:3, :3]


def shape(*dims, dtype=F32):
    return jax.ShapeDtypeStruct(dims, dtype)


def in_hbm(*arrays):
    return [pltpu.with_memory_space_constraint(x, pltpu.HBM) for x in arrays]


def params():
    return pltpu.CompilerParams(vmem_limit_bytes=48 * 1024 * 1024)


def body(
    positions,
    species,
    site_atom,
    edge_center,
    edge_other,
    edge_count,
    w_in,
    w_two,
    w_env,
    w_value,
    w_latent,
    w_out,
    readout,
):
    half = (4, LANES)
    hbm = pl.BlockSpec(memory_space=pltpu.HBM)
    inputs = (
        site_atom,
        jnp.transpose(positions, (1, 0, 2)),
        species,
        edge_center,
        edge_other,
        w_in.T,
        w_two,
        w_env,
        w_value,
        w_latent,
        w_out,
        readout.reshape(1, 64),
        jnp.asarray(ROUTES, BF16),
    )
    own, first, second, hot, *copied, routes = pl.pallas_call(
        send_kernel,
        in_specs=[hbm] * len(inputs),
        out_shape=(shape(*half), shape(2, LANES), shape(2, LANES), shape(ATOMS, LANES, dtype=BF16))
        + tuple(shape(*x.shape, dtype=x.dtype) for x in inputs[1:]),
        scratch_shapes=[pltpu.VMEM((1, ATOMS), jnp.int32), pltpu.SemaphoreType.DMA((len(inputs),))],
        compiler_params=params(),
        name="sites",
    )(*in_hbm(*inputs))
    first = lax.ppermute(first, "gz", [(i, ((i - 1) ^ 1) + 1 & 7) for i in range(COUNT)])
    second = lax.ppermute(second, "gz", [(i, i ^ 1) for i in range(COUNT)])

    vmem = pl.BlockSpec(memory_space=pltpu.VMEM)
    prepared = pl.pallas_call(
        prepare_kernel,
        in_specs=[pl.BlockSpec(memory_space=pltpu.SMEM)] + [vmem] * 11,
        out_shape=(
            shape(1, EDGES, dtype=jnp.int32),
            shape(1, EDGES),
            shape(8, 256),
            shape(8, 512),
            shape(256, 32, dtype=BF16),
            shape(384, 256, dtype=BF16),
            shape(256, 512, dtype=BF16),
            shape(512, 256, dtype=BF16),
            shape(256, 384, dtype=BF16),
            shape(32, 256, dtype=BF16),
            shape(128, LANES),
        ),
        compiler_params=params(),
        cost_estimate=pl.CostEstimate(flops=10_000_000, bytes_accessed=2_000_000, transcendentals=0),
        name="slots_and_weights",
    )(edge_count, *copied)

    planes = (COUNT * COUNT, LANES)
    column, outer = pl.pallas_call(
        column_kernel,
        out_shape=(shape(*planes), shape(*half)),
        compiler_params=params(),
        name="column",
    )(own, first, second, routes, prepared[3])
    arrived = lax.all_to_all(column, ("gx", "gy"), 0, 0)

    message, extended_grad, local_grad = pl.pallas_call(
        main_kernel,
        out_shape=(shape(*planes), shape(4, 256), shape(8, ATOMS)),
        scratch_shapes=[
            pltpu.VMEM((512, EDGES), BF16),
            pltpu.VMEM((8, 8, EDGES), F32),
            pltpu.VMEM((8, EDGES), F32),
            pltpu.VMEM((16, 8, EDGES), F32),
            pltpu.VMEM((16, 8, EDGES), F32),
            pltpu.VMEM((256, EDGES), BF16),
            pltpu.VMEM((512, EDGES), BF16),
            pltpu.VMEM((24, 8, EDGES), F32),
            pltpu.VMEM((2, 8, 8, EDGES), F32),
            pltpu.VMEM((9, 8, 8, 256), F32),
            pltpu.VMEM((32, 8, EDGES), F32),
            pltpu.VMEM((8, 8, EDGES), F32),
            pltpu.VMEM((8, EDGES), F32),
            pltpu.VMEM((8, EDGES), F32),
        ],
        compiler_params=params(),
        name="edges",
    )(arrived, outer, own, *prepared)
    returned = lax.all_to_all(message, ("gx", "gy"), 0, 0)
    layers, keep = pl.pallas_call(
        middle_kernel,
        out_shape=(shape(COUNT, 4, LANES), shape(8, LANES)),
        compiler_params=params(),
        name="columns_back",
    )(returned, extended_grad, routes)
    closing = lax.all_to_all(layers, "gz", 0, 0)
    forces, site_energy, virial = pl.pallas_call(
        last_kernel,
        out_shape=(shape(3, 1, ATOMS), shape(1, ATOMS), shape(3, 3)),
        compiler_params=params(),
        name="forces",
    )(closing, keep, local_grad, hot)
    return jnp.transpose(forces, (1, 0, 2)), site_energy, virial


def solution(mesh):
    by_domain = ("gx", "gy", "gz")
    placed = (
        P(by_domain, None, None),
        P(by_domain, None),
        P(by_domain, None),
        P(by_domain, None),
        P(by_domain, None),
        P(by_domain),
    ) + (P(),) * 7
    return jax.shard_map(
        body,
        mesh=mesh,
        in_specs=placed,
        out_specs=(P(by_domain, None, None), P(by_domain, None), P()),
        check_vma=False,
    )
```

```python
import math

import jax
import jax.numpy as jnp
import numpy as np
from jax import lax
from jax.experimental import pallas as pl
from jax.experimental.pallas import tpu as pltpu
from jax.sharding import PartitionSpec as P

CELLS = 6
LAYERS = 2
ATOMS = 72
EDGES = 1152
BLOCKS = 9
LANES = 128
MAIN = 64
COUNT = 8
F32 = jnp.float32
BF16 = jnp.bfloat16
HIGHEST = lax.Precision.HIGHEST
ROOT3 = math.sqrt(3.0)
RING = 28
STEPS = [(dx, dy) for dx in (-1, 0, 1) for dy in (-1, 0, 1) if (dx, dy) != (0, 0)]


SITE_RANGE = {1: [5], -1: [0], 0: list(range(6))}
def face(dx, dy):
    return list(enumerate((x, y) for x in SITE_RANGE[dx] for y in SITE_RANGE[dy]))


def tables():
    routes = np.zeros((256, 256), np.float32)
    layers = {0: 0, 3: 64, 1: LANES, 2: LANES + 64}
    for k in range(4):
        for n, (dx, dy) in enumerate(STEPS):
            for m, (x, y) in face(dx, dy):
                routes[layers[k] + x * 6 + y, n * 32 + k * 8 + m] = 1.0
    return routes


ROUTES = tables()


def parts_of(x, count):
    found = []
    for _ in range(count - 1):
        part = x.astype(BF16).astype(F32)
        found.append(part)
        x = x - part
    found.append(x)
    return found


def split_rows(x, count):
    return jnp.concatenate(parts_of(x, count), axis=0).astype(BF16)


def exact_dot(x, table, count=3):
    rows = x.shape[0]
    out = jnp.dot(split_rows(x, count), table, preferred_element_type=F32)
    return sum(out[i * rows : (i + 1) * rows] for i in range(1, count)) + out[:rows]


def exact_dot_nt(x, table, count=3):
    rows = x.shape[0]
    out = lax.dot_general(split_rows(x, count), table, (((1,), (1,)), ((), ())), preferred_element_type=F32)
    return sum(out[i * rows : (i + 1) * rows] for i in range(1, count)) + out[:rows]


def pad_rows(x):
    return jnp.concatenate([x, jnp.zeros((8 - x.shape[0], x.shape[1]), F32)], axis=0)


def iota(shape, dim):
    return lax.broadcasted_iota(jnp.int32, shape, dim)


def as_hot(mask):
    return jnp.where(mask, 1.0, 0.0).astype(BF16)


def start_fetch(sources, buffers, sems):
    copies = [pltpu.make_async_copy(src, dst, sems.at[n]) for n, (src, dst) in enumerate(zip(sources, buffers))]
    for copy in copies:
        copy.start()
    return copies


def atom_rows(pos_ref, kind_ref):
    kind = kind_ref[...].astype(F32)
    return jnp.concatenate([pos_ref[0], pos_ref[1], pos_ref[2], kind, jnp.zeros((4, ATOMS), F32)], axis=0)


def lane_sites():
    lane = iota((8, LANES), 1)
    at = lane & 63
    return jnp.where(at < 36, 2 * at + (lane >> 6), -1)


def pick_lanes(x, lanes):
    return jnp.take_along_axis(x, lanes, axis=1, mode="promise_in_bounds")


def low_half(x, y):
    return jnp.where(iota(x.shape, 1) < 64, x, y)


def even_layer():
    return (lax.axis_index("gz") & 1) == 0


def send_kernel(*refs):
    sources, (both_ref, first_ref, second_ref, hot_ref), copied = refs[:10], refs[10:14], refs[14:23]
    pos_ref, kind_ref, site_ref = copied[0], copied[1], refs[23]
    copies = start_fetch(sources, (site_ref,) + copied, refs[24])
    for copy in copies[:3]:
        copy.wait()
    rows = atom_rows(pos_ref, kind_ref)
    sites = lane_sites()
    wide = jnp.concatenate([site_ref[...], jnp.zeros((1, LANES - ATOMS), jnp.int32)], axis=1)
    atoms = pick_lanes(jnp.broadcast_to(wide, (8, LANES)), jnp.maximum(sites, 0))
    both = pick_lanes(jnp.concatenate([rows, jnp.zeros((8, LANES - ATOMS), F32)], axis=1), atoms)
    both = jnp.where(sites >= 0, both, 0.0)
    turned = pltpu.roll(both, 64, 1)
    down = [low_half(both[c : c + 1], turned[c + 1 : c + 2]) for c in (0, 2)]
    up = [low_half(turned[c : c + 1], both[c + 1 : c + 2]) for c in (0, 2)]
    for c in range(2):
        first_ref[c : c + 1] = jnp.where(even_layer(), down[c], up[c])
        second_ref[c : c + 1] = jnp.where(even_layer(), up[c], down[c])
    both_ref[...] = both[:4]
    hot_ref[...] = as_hot(iota((ATOMS, LANES), 0) == jnp.where(sites >= 0, atoms, -1)[0:1])
    for copy in copies[3:]:
        copy.wait()


def on_component():
    return (iota((8, LANES), 1) >> 5) == iota((8, LANES), 0)


def turn(x, step):
    comp = iota((8, LANES), 0)
    out = x
    for c in range(1, 4):
        out = jnp.where(comp == c, pltpu.roll(x, c * step % LANES, 1), out)
    return out


def from_rows(rows):
    halves = []
    for h in range(2):
        total = jnp.zeros((8, LANES), F32)
        for m in range(4):
            part = jnp.where(on_component(), jnp.broadcast_to(rows[4 * h + m], (8, LANES)), 0.0)
            total = total + (pltpu.roll(part, 32 * m, 1) if m else part)
        halves.append(turn(total, -32))
    return halves


def to_rows(x):
    rows = []
    for h in range(2):
        turned = turn(x[:, h * LANES : (h + 1) * LANES], 32)
        for m in range(4):
            part = pltpu.roll(turned, LANES - 32 * m, 1) if m else turned
            rows.append(jnp.sum(jnp.where(on_component(), part, 0.0), axis=0, keepdims=True))
    return rows


def neighbour(n):
    dx, dy = STEPS[n]
    gx = lax.axis_index("gx")
    gy = lax.axis_index("gy")
    return lax.rem(gx + (dx + COUNT), COUNT) * COUNT + lax.rem(gy + (dy + COUNT), COUNT)


def column_kernel(inner_ref, first_ref, second_ref, routes_ref, msg_ref, outer_ref):
    first, second = first_ref[...], second_ref[...]
    below = jnp.where(even_layer(), first, second)
    above = jnp.where(even_layer(), second, first)
    below_turned, above_turned = pltpu.roll(below, 64, 1), pltpu.roll(above, 64, 1)
    rows = []
    for c in range(2):
        at = slice(c, c + 1)
        rows += [low_half(below[at], above_turned[at]), low_half(below_turned[at], above[at])]
    outer = pad_rows(jnp.concatenate(rows, axis=0))
    outer_ref[...] = outer[:4]
    column = jnp.concatenate([outer, pad_rows(inner_ref[...])], axis=1)
    rows = to_rows(exact_dot(column, routes_ref[...]))
    msg_ref[...] = jnp.zeros_like(msg_ref)
    for n in range(8):
        msg_ref[pl.ds(neighbour(n), 1), :] = rows[n]


def cat_of(w):
    high = w.astype(BF16).astype(F32)
    low = w - high
    both = jnp.concatenate([high, low], axis=0)
    return jnp.concatenate([both, both], axis=1).astype(BF16)


def dot_cat(w, x):
    out = jnp.dot(w, x, preferred_element_type=F32)
    rows = out.shape[0] // 2
    return out[:rows] + out[rows:]


def cell_shifts():
    lane = iota((8, 512), 1)
    row = iota((8, 512), 0)
    outer = lane < 256
    code = lane >> 5
    code = code + jnp.where(code >= 4, 1, 0)
    third = jnp.where(code >= 3, 1, 0) + jnp.where(code >= 6, 1, 0)
    along_x = jnp.where(outer, third - 1, 0)
    along_y = jnp.where(outer, code - 3 * third - 1, 0)
    layer = (lane >> 3) & 3
    part = lane >> 6
    low_z = jnp.where(outer, layer, part - 4) == 0
    high_z = jnp.where(outer, layer, part - 2) == 3
    along_z = jnp.where(high_z, 1, 0) - jnp.where(low_z, 1, 0)
    shift = jnp.where(row == 0, 12 * along_x, jnp.where(row == 1, 12 * along_y, 4 * along_z))
    return jnp.where(row < 3, shift, 0).astype(F32)


def prepare_kernel(count_ref, *refs):
    inputs, sources, outputs, buffers, sems = refs[:9], refs[9:12], refs[12:24], refs[24:26], refs[26]
    copies = start_fetch(sources, buffers + outputs[11:], sems)
    make_slots(count_ref, inputs[:4], outputs[:4])
    for copy in copies[:2]:
        copy.wait()
    make_weights(inputs[4:] + buffers, outputs[4:11])
    copies[2].wait()


def make_slots(count_ref, buffers, outputs):
    pos_ref, kind_ref, center_ref, other_ref = buffers
    cell_ref, live_ref, own_ref, shift_ref = outputs
    shift_ref[...] = cell_shifts()
    before = as_hot((iota((LANES, 256), 0) < iota((LANES, 256), 1)) | (iota((LANES, 256), 1) >= LANES))
    lane = iota((ATOMS, 256), 1)
    spread = as_hot(iota((ATOMS, 256), 0) == jnp.where(lane < LANES, lane & 63, MAIN + (lane & 7)))
    center = center_ref[...]
    other = other_ref[...]
    atom = lax.broadcasted_iota(jnp.int32, (ATOMS, EDGES), 0)
    hot = jnp.where(atom == center, 1.0, 0.0)
    hot16 = hot.astype(BF16)
    running = jnp.zeros((ATOMS, LANES), F32)
    ranks = []
    for b in range(BLOCKS):
        at = slice(b * LANES, (b + 1) * LANES)
        sums = jnp.dot(hot16[:, at], before, preferred_element_type=F32)
        ranks.append(jnp.sum(hot[:, at] * (sums[:, :LANES] + running), axis=0, keepdims=True))
        running = running + sums[:, LANES:]
    rank = jnp.concatenate(ranks, axis=1).astype(jnp.int32)
    is_main = center < MAIN
    block = jnp.where(is_main, rank >> 1, BLOCKS - 1)
    lane = jnp.where(is_main, (rank & 1) * MAIN + center, rank * 8 + (center - MAIN))
    i, j, k = other >> 5, (other >> 2) & 7, other & 3
    dx = jnp.where(i == 7, 1, 0) - jnp.where(i == 0, 1, 0)
    dy = jnp.where(j == 7, 1, 0) - jnp.where(j == 0, 1, 0)
    code = 3 * dx + dy + 4
    place = jnp.where(dx == 0, i - 1, 0) + jnp.where(dy == 0, j - 1, 0)
    layer = jnp.where(k == 3, 64, jnp.where(k > 0, 64 * k + 64, 0))
    cell = jnp.where(
        code == 4,
        256 + layer + (i - 1) * 6 + (j - 1),
        (code - jnp.where(code > 4, 1, 0)) * 32 + k * 8 + place,
    )
    slot = lax.broadcasted_iota(jnp.int32, (1, EDGES), 1)
    live = jnp.where(slot < count_ref[0], 1.0, 0.0)
    row = lax.broadcasted_iota(jnp.int32, (16, EDGES), 0)
    values = ((cell & 255).astype(F32), (cell >> 8).astype(F32), live)
    left = jnp.concatenate([jnp.where(row == block, v, 0.0) for v in values], axis=0)
    lane_hot = jnp.where(lax.broadcasted_iota(jnp.int32, (LANES, EDGES), 0) == lane, 1.0, 0.0).astype(BF16)
    placed = lax.dot_general(
        left.astype(BF16), lane_hot, (((1,), (1,)), ((), ())), preferred_element_type=F32
    )
    for b in range(BLOCKS):
        at = slice(b * LANES, (b + 1) * LANES)
        cell_ref[:, at] = (placed[b : b + 1] + 256.0 * placed[16 + b : 17 + b]).astype(jnp.int32)
        live_ref[:, at] = placed[32 + b : 33 + b]
    own_ref[...] = exact_dot(atom_rows(pos_ref, kind_ref), spread)


def make_weights(buffers, outputs):
    win_ref, w3_ref, wlat_ref, wlat_t_ref, w3_t_ref, win_t_ref, read_ref = outputs
    w_out_ref, readout_ref, w_two_ref, w_env_ref, w_value_ref, w_latent_ref, w_in_ref = buffers
    w_in_t = w_in_ref[...]
    win_ref[...] = cat_of(w_in_t.T)
    w_two = w_two_ref[...]
    mixed = jnp.concatenate([w_env_ref[...], w_value_ref[...]], axis=0)
    w3 = jnp.concatenate(
        [w_two, jnp.dot(mixed, w_two, precision=HIGHEST, preferred_element_type=F32)], axis=0
    )
    w3_ref[...] = cat_of(w3)
    w3_t_ref[...] = cat_of(w3.T)
    w_latent = w_latent_ref[...]
    wlat_ref[...] = cat_of(w_latent)
    wlat_t_ref[...] = cat_of(w_latent.T)
    win_t_ref[...] = cat_of(w_in_t)
    square = lax.broadcasted_iota(jnp.int32, (64, 64), 0) == lax.broadcasted_iota(jnp.int32, (64, 64), 1)
    column = jnp.sum(jnp.where(square, readout_ref[...], 0.0), axis=1, keepdims=True)
    read_ref[...] = jnp.dot(
        w_out_ref[...].T,
        jnp.broadcast_to(column, (64, LANES)),
        precision=HIGHEST,
        preferred_element_type=F32,
    )


def cos_sin_pi(t):
    whole = jnp.floor(t + 0.5)
    f = t - whole
    half = whole * 0.5
    sign = 1.0 - 4.0 * (half - jnp.floor(half))
    a = f * math.pi
    q = a * a
    c = 1.0 + q * (
        -0.5
        + q * (1 / 24 + q * (-1 / 720 + q * (1 / 40320 + q * (-1 / 3628800 + q * (1 / 479001600)))))
    )
    s = a * (
        1.0
        + q
        * (-1 / 6 + q * (1 / 120 + q * (-1 / 5040 + q * (1 / 362880 + q * (-1 / 39916800 + q * (1 / 6227020800))))))
    )
    return c * sign, s * sign


def sum_slots(main, last):
    main = main + pltpu.roll(main, 64, 1)
    for shift in (64, 32, 16, 8):
        last = last + pltpu.roll(last, shift, 1)
    return main, last


def store_cat(ref, row, depth, at, x):
    high = x.astype(BF16)
    low = (x - high.astype(F32)).astype(BF16)
    ref[pl.ds(row, 16), at] = high
    ref[pl.ds(depth + row, 16), at] = low


def repeat(count, step):
    for n in range(count):
        step(n, 0)


def main_kernel(
    recv_ref,
    outer_ref,
    inner_ref,
    cell_ref,
    live_ref,
    own_ref,
    shift_ref,
    win_ref,
    w3_ref,
    wlat_ref,
    wlat_t_ref,
    w3_t_ref,
    win_t_ref,
    read_ref,
    msg_ref,
    ext_ref,
    local_ref,
    hot,
    harm,
    env_live,
    pre,
    slope,
    cat_a,
    cat_b,
    mixed,
    paths,
    environment,
    grad_lat,
    grad_harm,
    grad_env,
    energy,
):
    blocks = [slice(b * LANES, (b + 1) * LANES) for b in range(BLOCKS)]

    columns = from_rows([recv_ref[pl.ds(neighbour(n), 1), :] for n in range(8)])
    columns += [pad_rows(outer_ref[...]), pad_rows(inner_ref[...])]
    extended = jnp.concatenate(columns, axis=1) + shift_ref[...]
    cells = lax.broadcasted_iota(jnp.int32, (512, EDGES), 0)
    hot[...] = jnp.where(cells == cell_ref[...], 1.0, 0.0).astype(BF16)
    partner = exact_dot(extended, hot[...])
    own = own_ref[...]
    center = jnp.concatenate([own[:, :LANES]] * 8 + [own[:, LANES:]], axis=1)
    displacement = partner - center

    def wide(x, row):
        return jnp.broadcast_to(x[row : row + 1], (8, EDGES))

    x = wide(displacement, 0) * 0.2
    y = wide(displacement, 1) * 0.2
    z = wide(displacement, 2) * 0.2
    scaled = x * x + y * y + z * z
    live = jnp.broadcast_to(live_ref[...], (8, EDGES))
    env_live[...] = (1.0 - scaled) * (1.0 - scaled) * live
    harm[0] = x
    harm[1] = y
    harm[2] = z
    harm[3] = ROOT3 * x * y
    harm[4] = ROOT3 * y * z
    harm[5] = ROOT3 * x * z
    harm[6] = (0.5 * ROOT3) * (x * x - y * y)
    harm[7] = 0.5 * (2.0 * z * z - x * x - y * y)

    order = lax.broadcasted_iota(jnp.int32, (8, EDGES), 0)
    orders = order.astype(F32)
    radial, radial_sin = cos_sin_pi(orders * scaled)
    kinds = jnp.where(order < 4, wide(center, 3), wide(partner, 3) + 4.0)
    one_hot = jnp.where(kinds == orders, 1.0, 0.0)
    inputs = jnp.concatenate([radial, one_hot], axis=0)
    inputs_high = inputs.astype(BF16)
    inputs_low = (inputs - inputs_high.astype(F32)).astype(BF16)
    pre[...] = dot_cat(win_ref[...], jnp.concatenate([inputs_high, inputs_low], axis=0)).reshape(16, 8, EDGES)

    def first_layer(c, carry):
        v = pre[pl.ds(2 * c, 2)]
        gate = 1.0 / (1.0 + jnp.exp(-v))
        out = v * gate
        slope[pl.ds(2 * c, 2)] = gate + out * (1.0 - gate)
        store_cat(cat_a, 16 * c, 128, slice(None), out.reshape(16, EDGES))
        return carry

    repeat(8, first_layer)
    mixed[...] = dot_cat(w3_ref[...], cat_a[...]).reshape(24, 8, EDGES)

    def forward_tile(t, carry):
        sums = [[None, None] for _ in range(9)]
        for b, at in enumerate(blocks):
            weight = mixed[pl.ds(8 + 2 * t, 2), :, at] * env_live[:, at]
            part = 0 if b < 8 else 1
            for r in range(9):
                term = weight if r == 0 else weight * harm[r - 1, :, at]
                sums[r][part] = term if sums[r][part] is None else sums[r][part] + term
        found = []
        for r in range(9):
            main, last = sum_slots(sums[r][0].reshape(16, LANES), sums[r][1].reshape(16, LANES))
            main, last = main.reshape(2, 8, LANES), last.reshape(2, 8, LANES)
            environment[r, pl.ds(2 * t, 2), :, 0:LANES] = main
            environment[r, pl.ds(2 * t, 2), :, LANES : 2 * LANES] = last
            found.append((main, last))
        for b, at in enumerate(blocks):
            part = 0 if b < 8 else 1
            h = [None] + [harm[r, :, at] for r in range(8)]
            e = [found[r][part] for r in range(9)]
            one = h[1] * e[1] + h[2] * e[2] + h[3] * e[3]
            two = h[4] * e[4] + h[5] * e[5] + h[6] * e[6] + h[7] * e[7] + h[8] * e[8]
            paths[0, pl.ds(2 * t, 2), :, at] = one
            paths[1, pl.ds(2 * t, 2), :, at] = two
            values = mixed[pl.ds(16 + 2 * t, 2), :, at]
            base = 16 * t
            store_cat(cat_b, base, 256, at, mixed[pl.ds(2 * t, 2), :, at].reshape(16, LANES))
            store_cat(cat_b, 64 + base, 256, at, (e[0] * values).reshape(16, LANES))
            store_cat(cat_b, 128 + base, 256, at, (one * values).reshape(16, LANES))
            store_cat(cat_b, 192 + base, 256, at, (two * values).reshape(16, LANES))
        return carry

    repeat(4, forward_tile)
    pre[...] = dot_cat(wlat_ref[...], cat_b[...]).reshape(16, 8, EDGES)
    energy[...] = jnp.zeros((8, EDGES), F32)

    def second_layer(c, carry):
        v = pre[pl.ds(2 * c, 2)]
        gate = 1.0 / (1.0 + jnp.exp(-v))
        out = v * gate
        weights = read_ref[pl.ds(16 * c, 16), :].reshape(2, 8, LANES)
        weights = jnp.concatenate([weights] * BLOCKS, axis=2)
        product = weights * out
        energy[...] += product[0] + product[1]
        back = weights * (gate + out * (1.0 - gate)) * env_live[...]
        store_cat(cat_a, 16 * c, 128, slice(None), back.reshape(16, EDGES))
        return carry

    repeat(8, second_layer)
    grad_lat[...] = dot_cat(wlat_t_ref[...], cat_a[...]).reshape(32, 8, EDGES)
    grad_harm[...] = jnp.zeros((8, 8, EDGES), F32)
    grad_env[...] = jnp.zeros((8, EDGES), F32)

    def backward_tile(t, carry):
        base = 16 * t
        sums = [[None, None] for _ in range(9)]
        for b, at in enumerate(blocks):
            part = 0 if b < 8 else 1
            lanes = slice(part * LANES, (part + 1) * LANES)
            values = mixed[pl.ds(16 + 2 * t, 2), :, at]
            d = [grad_lat[pl.ds(8 + 8 * l + 2 * t, 2), :, at] for l in range(3)]
            zero = environment[0, pl.ds(2 * t, 2), :, lanes]
            one = paths[0, pl.ds(2 * t, 2), :, at]
            two = paths[1, pl.ds(2 * t, 2), :, at]
            d_values = d[0] * zero + d[1] * one + d[2] * two
            store_cat(cat_b, 128 + base, 192, at, d_values.reshape(16, LANES))
            store_cat(cat_b, base, 192, at, grad_lat[pl.ds(2 * t, 2), :, at].reshape(16, LANES))
            q = [d[l] * values for l in range(3)]
            for r in range(9):
                level = 0 if r == 0 else (1 if r < 4 else 2)
                term = q[0] if r == 0 else q[level] * harm[r - 1, :, at]
                sums[r][part] = term if sums[r][part] is None else sums[r][part] + term
        found = []
        for r in range(9):
            main, last = sum_slots(sums[r][0].reshape(16, LANES), sums[r][1].reshape(16, LANES))
            found.append((main.reshape(2, 8, LANES), last.reshape(2, 8, LANES)))
        for b, at in enumerate(blocks):
            part = 0 if b < 8 else 1
            lanes = slice(part * LANES, (part + 1) * LANES)
            raw = mixed[pl.ds(8 + 2 * t, 2), :, at]
            envelope = env_live[:, at]
            weight = raw * envelope
            values = mixed[pl.ds(16 + 2 * t, 2), :, at]
            q = [None] + [grad_lat[pl.ds(8 + 8 * l + 2 * t, 2), :, at] * values for l in (1, 2)]
            d_weight = found[0][part]
            for r in range(1, 9):
                g = found[r][part]
                d_weight = d_weight + harm[r - 1, :, at] * g
                level = 1 if r < 4 else 2
                term = q[level] * environment[r, pl.ds(2 * t, 2), :, lanes] + weight * g
                grad_harm[r - 1, :, at] += term[0] + term[1]
            slack = d_weight * raw
            grad_env[:, at] += slack[0] + slack[1]
            store_cat(cat_b, 64 + base, 192, at, (d_weight * envelope).reshape(16, LANES))
        return carry

    repeat(4, backward_tile)
    pre[...] = dot_cat(w3_t_ref[...], cat_b[0:384]).reshape(16, 8, EDGES)

    def first_back(c, carry):
        back = pre[pl.ds(2 * c, 2)] * slope[pl.ds(2 * c, 2)]
        store_cat(cat_a, 16 * c, 128, slice(None), back.reshape(16, EDGES))
        return carry

    repeat(8, first_back)
    d_radial = dot_cat(win_t_ref[...], cat_a[...])[:8]

    x, y, z = harm[0], harm[1], harm[2]
    scaled = x * x + y * y + z * z
    live = jnp.broadcast_to(live_ref[...], (8, EDGES))
    d_scaled = d_radial * (orders * radial_sin) * (-math.pi) + (grad_env[...] + energy[...]) * (
        -2.0 * (1.0 - scaled) * live
    )
    g = [grad_harm[r] for r in range(8)]
    twice = 2.0 * d_scaled
    d_x = g[0] + ROOT3 * (y * g[3] + z * g[5] + x * g[6]) - x * g[7] + twice * x
    d_y = g[1] + ROOT3 * (x * g[3] + z * g[4] - y * g[6]) - y * g[7] + twice * y
    d_z = g[2] + ROOT3 * (y * g[4] + x * g[5]) + 2.0 * z * g[7] + twice * z
    e = energy[...] * env_live[...]
    partial = [d_x * 0.2, d_y * 0.2, d_z * 0.2]
    extended_grad = exact_dot_nt(jnp.concatenate(partial, axis=0), hot[...], 2)

    def over_blocks(v):
        total = v[:, blocks[0]]
        for b in range(1, 8):
            total = total + v[:, blocks[b]]
        return total

    def summed(arrays):
        rows = [jnp.sum(v, axis=0, keepdims=True) for v in arrays]
        return jnp.concatenate(rows + [jnp.zeros((8 - len(rows), rows[0].shape[1]), F32)], axis=0)

    virial = []
    for a, comp in enumerate((x, y, z)):
        for b in range(3):
            product = comp * partial[b]
            virial.append(over_blocks(product) + product[:, blocks[8]])
    totals = jnp.sum(jnp.concatenate(virial, axis=0), axis=1, keepdims=True)
    lane = lax.broadcasted_iota(jnp.int32, (8, LANES), 1)
    virial = jnp.zeros((8, LANES), F32)
    for n in range(9):
        virial = jnp.where(lane == 96 + n, totals[8 * n : 8 * n + 8] * 5.0, virial)
    virial = jnp.sum(virial, axis=0, keepdims=True)

    extended_grad = summed([extended_grad[8 * c : 8 * c + 8] for c in range(3)])
    rows = to_rows(extended_grad[:, :256])
    msg_ref[...] = jnp.broadcast_to(virial, (COUNT * COUNT, LANES))
    for n in range(8):
        msg_ref[pl.ds(neighbour(n), 1), :] = rows[n] + virial
    ext_ref[...] = extended_grad[:4, 256:]

    arrays = partial + [e]
    main, last = sum_slots(summed([over_blocks(v) for v in arrays]), summed([v[:, blocks[8]] for v in arrays]))
    local_ref[...] = jnp.concatenate([main[:, :MAIN], last[:, : ATOMS - MAIN]], axis=1)


def middle_kernel(recv_ref, ext_ref, routes_ref, msg_ref, keep_ref):
    columns = from_rows([recv_ref[pl.ds(neighbour(n), 1), :] for n in range(8)])
    sums = exact_dot_nt(jnp.concatenate(columns, axis=1), routes_ref[...], 2) + pad_rows(ext_ref[...])
    total = jnp.sum(recv_ref[...], axis=0, keepdims=True)
    message = jnp.concatenate([sums[:3, :LANES], total], axis=0)
    msg_ref[...] = jnp.broadcast_to(message[None], (COUNT, 4, LANES))
    keep_ref[...] = sums[:, LANES:]


def last_kernel(recv_ref, keep_ref, local_ref, hot_ref, force_ref, energy_ref, virial_ref):
    gz = lax.axis_index("gz")
    above = pad_rows(recv_ref[lax.rem(gz + 1, COUNT)])
    below = pad_rows(recv_ref[lax.rem(gz + (COUNT - 1), COUNT)])
    lane = lax.broadcasted_iota(jnp.int32, (8, LANES), 1)
    row = lax.broadcasted_iota(jnp.int32, (8, LANES), 0)
    sites = keep_ref[...] + jnp.where(lane < 64, pltpu.roll(below, 64, 1), pltpu.roll(above, 64, 1))
    atoms = exact_dot_nt(sites, hot_ref[...], 2)
    energy_ref[...] = local_ref[3:4]
    force = local_ref[...] - atoms
    for comp in range(3):
        force_ref[comp] = force[comp : comp + 1]
    total = jnp.broadcast_to(jnp.sum(recv_ref[...], axis=0)[3:4], (8, LANES))
    normalizer = -1.0 / math.sqrt(EDGES * COUNT * COUNT * COUNT)
    virial = jnp.zeros((8, LANES), F32)
    for b in range(3):
        entry = jnp.sum(jnp.where(lane == 96 + 3 * row + b, total, 0.0), axis=1, keepdims=True)
        virial = jnp.where(lane == b, entry * normalizer, virial)
    virial_ref[...] = virial[:3, :3]


def shape(*dims, dtype=F32):
    return jax.ShapeDtypeStruct(dims, dtype)


def in_hbm(*arrays):
    return [pltpu.with_memory_space_constraint(x, pltpu.HBM) for x in arrays]


def params():
    return pltpu.CompilerParams(vmem_limit_bytes=48 * 1024 * 1024)


def body(
    positions,
    species,
    site_atom,
    edge_center,
    edge_other,
    edge_count,
    w_in,
    w_two,
    w_env,
    w_value,
    w_latent,
    w_out,
    readout,
):
    half = (4, LANES)
    hbm = pl.BlockSpec(memory_space=pltpu.HBM)
    inputs = (
        site_atom,
        jnp.transpose(positions, (1, 0, 2)),
        species,
        edge_center,
        edge_other,
        w_out,
        readout.reshape(1, 64),
        w_two,
        w_env,
        w_value,
    )
    weights = (w_latent, w_in.T, jnp.asarray(ROUTES, BF16))
    own, first, second, hot, *copied = pl.pallas_call(
        send_kernel,
        in_specs=[hbm] * len(inputs),
        out_shape=(shape(*half), shape(2, LANES), shape(2, LANES), shape(ATOMS, LANES, dtype=BF16))
        + tuple(shape(*x.shape, dtype=x.dtype) for x in inputs[1:]),
        scratch_shapes=[pltpu.VMEM((1, ATOMS), jnp.int32), pltpu.SemaphoreType.DMA((len(inputs),))],
        compiler_params=params(),
        name="sites",
    )(*in_hbm(*inputs))
    first = lax.ppermute(first, "gz", [(i, ((i - 1) ^ 1) + 1 & 7) for i in range(COUNT)])
    second = lax.ppermute(second, "gz", [(i, i ^ 1) for i in range(COUNT)])

    vmem = pl.BlockSpec(memory_space=pltpu.VMEM)
    *prepared, routes = pl.pallas_call(
        prepare_kernel,
        in_specs=[pl.BlockSpec(memory_space=pltpu.SMEM)] + [vmem] * len(copied) + [hbm] * len(weights),
        out_shape=(
            shape(1, EDGES, dtype=jnp.int32),
            shape(1, EDGES),
            shape(8, 256),
            shape(8, 512),
            shape(256, 32, dtype=BF16),
            shape(384, 256, dtype=BF16),
            shape(256, 512, dtype=BF16),
            shape(512, 256, dtype=BF16),
            shape(256, 384, dtype=BF16),
            shape(32, 256, dtype=BF16),
            shape(128, LANES),
            shape(256, 256, dtype=BF16),
        ),
        scratch_shapes=[pltpu.VMEM(x.shape, x.dtype) for x in weights[:-1]]
        + [pltpu.SemaphoreType.DMA((len(weights),))],
        compiler_params=params(),
        cost_estimate=pl.CostEstimate(flops=10_000_000, bytes_accessed=2_000_000, transcendentals=0),
        name="slots_and_weights",
    )(edge_count, *copied, *in_hbm(*weights))

    planes = (COUNT * COUNT, LANES)
    column, outer = pl.pallas_call(
        column_kernel,
        out_shape=(shape(*planes), shape(*half)),
        compiler_params=params(),
        name="column",
    )(own, first, second, routes)
    arrived = lax.all_to_all(column, ("gx", "gy"), 0, 0)

    message, extended_grad, local_grad = pl.pallas_call(
        main_kernel,
        out_shape=(shape(*planes), shape(4, 256), shape(8, ATOMS)),
        scratch_shapes=[
            pltpu.VMEM((512, EDGES), BF16),
            pltpu.VMEM((8, 8, EDGES), F32),
            pltpu.VMEM((8, EDGES), F32),
            pltpu.VMEM((16, 8, EDGES), F32),
            pltpu.VMEM((16, 8, EDGES), F32),
            pltpu.VMEM((256, EDGES), BF16),
            pltpu.VMEM((512, EDGES), BF16),
            pltpu.VMEM((24, 8, EDGES), F32),
            pltpu.VMEM((2, 8, 8, EDGES), F32),
            pltpu.VMEM((9, 8, 8, 256), F32),
            pltpu.VMEM((32, 8, EDGES), F32),
            pltpu.VMEM((8, 8, EDGES), F32),
            pltpu.VMEM((8, EDGES), F32),
            pltpu.VMEM((8, EDGES), F32),
        ],
        compiler_params=params(),
        name="edges",
    )(arrived, outer, own, *prepared)
    returned = lax.all_to_all(message, ("gx", "gy"), 0, 0)
    layers, keep = pl.pallas_call(
        middle_kernel,
        out_shape=(shape(COUNT, 4, LANES), shape(8, LANES)),
        compiler_params=params(),
        name="columns_back",
    )(returned, extended_grad, routes)
    closing = lax.all_to_all(layers, "gz", 0, 0)
    forces, site_energy, virial = pl.pallas_call(
        last_kernel,
        out_shape=(shape(3, 1, ATOMS), shape(1, ATOMS), shape(3, 3)),
        compiler_params=params(),
        name="forces",
    )(closing, keep, local_grad, hot)
    return jnp.transpose(forces, (1, 0, 2)), site_energy, virial


def solution(mesh):
    by_domain = ("gx", "gy", "gz")
    placed = (
        P(by_domain, None, None),
        P(by_domain, None),
        P(by_domain, None),
        P(by_domain, None),
        P(by_domain, None),
        P(by_domain),
    ) + (P(),) * 7
    return jax.shard_map(
        body,
        mesh=mesh,
        in_specs=placed,
        out_specs=(P(by_domain, None, None), P(by_domain, None), P()),
        check_vma=False,
    )
```

```python
import math

import jax
import jax.numpy as jnp
import numpy as np
from jax import lax
from jax.experimental import pallas as pl
from jax.experimental.pallas import tpu as pltpu
from jax.sharding import PartitionSpec as P

CELLS = 6
LAYERS = 2
ATOMS = 72
EDGES = 1152
BLOCKS = 9
LANES = 128
MAIN = 64
COUNT = 8
F32 = jnp.float32
BF16 = jnp.bfloat16
HIGHEST = lax.Precision.HIGHEST
ROOT3 = math.sqrt(3.0)
RING = 28
STEPS = [(dx, dy) for dx in (-1, 0, 1) for dy in (-1, 0, 1) if (dx, dy) != (0, 0)]


SITE_RANGE = {1: [5], -1: [0], 0: list(range(6))}
def face(dx, dy):
    return list(enumerate((x, y) for x in SITE_RANGE[dx] for y in SITE_RANGE[dy]))


def tables():
    routes = np.zeros((256, 256), np.float32)
    layers = {0: 0, 3: 64, 1: LANES, 2: LANES + 64}
    for k in range(4):
        for n, (dx, dy) in enumerate(STEPS):
            for m, (x, y) in face(dx, dy):
                routes[layers[k] + x * 6 + y, n * 32 + k * 8 + m] = 1.0
    return routes


ROUTES = tables()


def parts_of(x, count):
    found = []
    for _ in range(count - 1):
        part = x.astype(BF16).astype(F32)
        found.append(part)
        x = x - part
    found.append(x)
    return found


def split_rows(x, count):
    return jnp.concatenate(parts_of(x, count), axis=0).astype(BF16)


def exact_dot(x, table, count=3):
    rows = x.shape[0]
    out = jnp.dot(split_rows(x, count), table, preferred_element_type=F32)
    return sum(out[i * rows : (i + 1) * rows] for i in range(1, count)) + out[:rows]


def exact_dot_nt(x, table, count=3):
    rows = x.shape[0]
    out = lax.dot_general(split_rows(x, count), table, (((1,), (1,)), ((), ())), preferred_element_type=F32)
    return sum(out[i * rows : (i + 1) * rows] for i in range(1, count)) + out[:rows]


def pad_rows(x):
    return jnp.concatenate([x, jnp.zeros((8 - x.shape[0], x.shape[1]), F32)], axis=0)


def iota(shape, dim):
    return lax.broadcasted_iota(jnp.int32, shape, dim)


def as_hot(mask):
    return jnp.where(mask, 1.0, 0.0).astype(BF16)


def start_fetch(sources, buffers, sems):
    copies = [pltpu.make_async_copy(src, dst, sems.at[n]) for n, (src, dst) in enumerate(zip(sources, buffers))]
    for copy in copies:
        copy.start()
    return copies


def atom_rows(pos_ref, kind_ref):
    kind = kind_ref[...].astype(F32)
    return jnp.concatenate([pos_ref[0], pos_ref[1], pos_ref[2], kind, jnp.zeros((4, ATOMS), F32)], axis=0)


def lane_sites():
    lane = iota((8, LANES), 1)
    at = lane & 63
    return jnp.where(at < 36, 2 * at + (lane >> 6), -1)


def pick_lanes(x, lanes):
    return jnp.take_along_axis(x, lanes, axis=1, mode="promise_in_bounds")


def low_half(x, y):
    return jnp.where(iota(x.shape, 1) < 64, x, y)


def even_layer():
    return (lax.axis_index("gz") & 1) == 0


def send_kernel(*refs):
    sources, (both_ref, first_ref, second_ref, hot_ref), copied = refs[:12], refs[12:16], refs[16:27]
    pos_ref, kind_ref, site_ref = copied[0], copied[1], refs[27]
    copies = start_fetch(sources, (site_ref,) + copied, refs[28])
    for copy in copies[:3]:
        copy.wait()
    rows = atom_rows(pos_ref, kind_ref)
    sites = lane_sites()
    wide = jnp.concatenate([site_ref[...], jnp.zeros((1, LANES - ATOMS), jnp.int32)], axis=1)
    atoms = pick_lanes(jnp.broadcast_to(wide, (8, LANES)), jnp.maximum(sites, 0))
    both = pick_lanes(jnp.concatenate([rows, jnp.zeros((8, LANES - ATOMS), F32)], axis=1), atoms)
    both = jnp.where(sites >= 0, both, 0.0)
    turned = pltpu.roll(both, 64, 1)
    down = [low_half(both[c : c + 1], turned[c + 1 : c + 2]) for c in (0, 2)]
    up = [low_half(turned[c : c + 1], both[c + 1 : c + 2]) for c in (0, 2)]
    for c in range(2):
        first_ref[c : c + 1] = jnp.where(even_layer(), down[c], up[c])
        second_ref[c : c + 1] = jnp.where(even_layer(), up[c], down[c])
    both_ref[...] = both[:4]
    hot_ref[...] = as_hot(iota((ATOMS, LANES), 0) == jnp.where(sites >= 0, atoms, -1)[0:1])
    for copy in copies[3:]:
        copy.wait()


def on_component():
    return (iota((8, LANES), 1) >> 5) == iota((8, LANES), 0)


def turn(x, step):
    comp = iota((8, LANES), 0)
    out = x
    for c in range(1, 4):
        out = jnp.where(comp == c, pltpu.roll(x, c * step % LANES, 1), out)
    return out


def from_rows(rows):
    halves = []
    for h in range(2):
        total = jnp.zeros((8, LANES), F32)
        for m in range(4):
            part = jnp.where(on_component(), jnp.broadcast_to(rows[4 * h + m], (8, LANES)), 0.0)
            total = total + (pltpu.roll(part, 32 * m, 1) if m else part)
        halves.append(turn(total, -32))
    return halves


def to_rows(x):
    rows = []
    for h in range(2):
        turned = turn(x[:, h * LANES : (h + 1) * LANES], 32)
        for m in range(4):
            part = pltpu.roll(turned, LANES - 32 * m, 1) if m else turned
            rows.append(jnp.sum(jnp.where(on_component(), part, 0.0), axis=0, keepdims=True))
    return rows


def neighbour(n):
    dx, dy = STEPS[n]
    gx = lax.axis_index("gx")
    gy = lax.axis_index("gy")
    return lax.rem(gx + (dx + COUNT), COUNT) * COUNT + lax.rem(gy + (dy + COUNT), COUNT)


def column_kernel(inner_ref, first_ref, second_ref, routes_ref, msg_ref, outer_ref):
    first, second = first_ref[...], second_ref[...]
    below = jnp.where(even_layer(), first, second)
    above = jnp.where(even_layer(), second, first)
    below_turned, above_turned = pltpu.roll(below, 64, 1), pltpu.roll(above, 64, 1)
    rows = []
    for c in range(2):
        at = slice(c, c + 1)
        rows += [low_half(below[at], above_turned[at]), low_half(below_turned[at], above[at])]
    outer = pad_rows(jnp.concatenate(rows, axis=0))
    outer_ref[...] = outer[:4]
    column = jnp.concatenate([outer, pad_rows(inner_ref[...])], axis=1)
    rows = to_rows(exact_dot(column, routes_ref[...]))
    msg_ref[...] = jnp.zeros_like(msg_ref)
    for n in range(8):
        msg_ref[pl.ds(neighbour(n), 1), :] = rows[n]


def cat_of(w):
    high = w.astype(BF16).astype(F32)
    low = w - high
    both = jnp.concatenate([high, low], axis=0)
    return jnp.concatenate([both, both], axis=1).astype(BF16)


def dot_cat(w, x):
    out = jnp.dot(w, x, preferred_element_type=F32)
    rows = out.shape[0] // 2
    return out[:rows] + out[rows:]


def cell_shifts():
    lane = iota((8, 512), 1)
    row = iota((8, 512), 0)
    outer = lane < 256
    code = lane >> 5
    code = code + jnp.where(code >= 4, 1, 0)
    third = jnp.where(code >= 3, 1, 0) + jnp.where(code >= 6, 1, 0)
    along_x = jnp.where(outer, third - 1, 0)
    along_y = jnp.where(outer, code - 3 * third - 1, 0)
    layer = (lane >> 3) & 3
    part = lane >> 6
    low_z = jnp.where(outer, layer, part - 4) == 0
    high_z = jnp.where(outer, layer, part - 2) == 3
    along_z = jnp.where(high_z, 1, 0) - jnp.where(low_z, 1, 0)
    shift = jnp.where(row == 0, 12 * along_x, jnp.where(row == 1, 12 * along_y, 4 * along_z))
    return jnp.where(row < 3, shift, 0).astype(F32)


def prepare_kernel(count_ref, *refs):
    inputs, table, outputs, sem = refs[:11], refs[11], refs[12:24], refs[24]
    copy = pltpu.make_async_copy(table, outputs[11], sem)
    copy.start()
    make_slots(count_ref, inputs[:4], outputs[:4])
    make_weights(inputs[4:], outputs[4:11])
    copy.wait()


def make_slots(count_ref, buffers, outputs):
    pos_ref, kind_ref, center_ref, other_ref = buffers
    cell_ref, live_ref, own_ref, shift_ref = outputs
    shift_ref[...] = cell_shifts()
    before = as_hot((iota((LANES, 256), 0) < iota((LANES, 256), 1)) | (iota((LANES, 256), 1) >= LANES))
    lane = iota((ATOMS, 256), 1)
    spread = as_hot(iota((ATOMS, 256), 0) == jnp.where(lane < LANES, lane & 63, MAIN + (lane & 7)))
    center = center_ref[...]
    other = other_ref[...]
    atom = lax.broadcasted_iota(jnp.int32, (ATOMS, EDGES), 0)
    hot = jnp.where(atom == center, 1.0, 0.0)
    hot16 = hot.astype(BF16)
    running = jnp.zeros((ATOMS, LANES), F32)
    ranks = []
    for b in range(BLOCKS):
        at = slice(b * LANES, (b + 1) * LANES)
        sums = jnp.dot(hot16[:, at], before, preferred_element_type=F32)
        ranks.append(jnp.sum(hot[:, at] * (sums[:, :LANES] + running), axis=0, keepdims=True))
        running = running + sums[:, LANES:]
    rank = jnp.concatenate(ranks, axis=1).astype(jnp.int32)
    is_main = center < MAIN
    block = jnp.where(is_main, rank >> 1, BLOCKS - 1)
    lane = jnp.where(is_main, (rank & 1) * MAIN + center, rank * 8 + (center - MAIN))
    i, j, k = other >> 5, (other >> 2) & 7, other & 3
    dx = jnp.where(i == 7, 1, 0) - jnp.where(i == 0, 1, 0)
    dy = jnp.where(j == 7, 1, 0) - jnp.where(j == 0, 1, 0)
    code = 3 * dx + dy + 4
    place = jnp.where(dx == 0, i - 1, 0) + jnp.where(dy == 0, j - 1, 0)
    layer = jnp.where(k == 3, 64, jnp.where(k > 0, 64 * k + 64, 0))
    cell = jnp.where(
        code == 4,
        256 + layer + (i - 1) * 6 + (j - 1),
        (code - jnp.where(code > 4, 1, 0)) * 32 + k * 8 + place,
    )
    slot = lax.broadcasted_iota(jnp.int32, (1, EDGES), 1)
    live = jnp.where(slot < count_ref[0], 1.0, 0.0)
    row = lax.broadcasted_iota(jnp.int32, (16, EDGES), 0)
    values = ((cell & 255).astype(F32), (cell >> 8).astype(F32), live)
    left = jnp.concatenate([jnp.where(row == block, v, 0.0) for v in values], axis=0)
    lane_hot = jnp.where(lax.broadcasted_iota(jnp.int32, (LANES, EDGES), 0) == lane, 1.0, 0.0).astype(BF16)
    placed = lax.dot_general(
        left.astype(BF16), lane_hot, (((1,), (1,)), ((), ())), preferred_element_type=F32
    )
    for b in range(BLOCKS):
        at = slice(b * LANES, (b + 1) * LANES)
        cell_ref[:, at] = (placed[b : b + 1] + 256.0 * placed[16 + b : 17 + b]).astype(jnp.int32)
        live_ref[:, at] = placed[32 + b : 33 + b]
    own_ref[...] = exact_dot(atom_rows(pos_ref, kind_ref), spread)


def make_weights(buffers, outputs):
    win_ref, w3_ref, wlat_ref, wlat_t_ref, w3_t_ref, win_t_ref, read_ref = outputs
    w_out_ref, readout_ref, w_two_ref, w_env_ref, w_value_ref, w_latent_ref, w_in_ref = buffers
    w_in_t = w_in_ref[...]
    win_ref[...] = cat_of(w_in_t.T)
    w_two = w_two_ref[...]
    mixed = jnp.concatenate([w_env_ref[...], w_value_ref[...]], axis=0)
    w3 = jnp.concatenate(
        [w_two, jnp.dot(mixed, w_two, precision=HIGHEST, preferred_element_type=F32)], axis=0
    )
    w3_ref[...] = cat_of(w3)
    w3_t_ref[...] = cat_of(w3.T)
    w_latent = w_latent_ref[...]
    wlat_ref[...] = cat_of(w_latent)
    wlat_t_ref[...] = cat_of(w_latent.T)
    win_t_ref[...] = cat_of(w_in_t)
    square = lax.broadcasted_iota(jnp.int32, (64, 64), 0) == lax.broadcasted_iota(jnp.int32, (64, 64), 1)
    column = jnp.sum(jnp.where(square, readout_ref[...], 0.0), axis=1, keepdims=True)
    read_ref[...] = jnp.dot(
        w_out_ref[...].T,
        jnp.broadcast_to(column, (64, LANES)),
        precision=HIGHEST,
        preferred_element_type=F32,
    )


def cos_sin_pi(t):
    whole = jnp.floor(t + 0.5)
    f = t - whole
    half = whole * 0.5
    sign = 1.0 - 4.0 * (half - jnp.floor(half))
    a = f * math.pi
    q = a * a
    c = 1.0 + q * (
        -0.5
        + q * (1 / 24 + q * (-1 / 720 + q * (1 / 40320 + q * (-1 / 3628800 + q * (1 / 479001600)))))
    )
    s = a * (
        1.0
        + q
        * (-1 / 6 + q * (1 / 120 + q * (-1 / 5040 + q * (1 / 362880 + q * (-1 / 39916800 + q * (1 / 6227020800))))))
    )
    return c * sign, s * sign


def sum_slots(main, last):
    main = main + pltpu.roll(main, 64, 1)
    for shift in (64, 32, 16, 8):
        last = last + pltpu.roll(last, shift, 1)
    return main, last


def store_cat(ref, row, depth, at, x):
    high = x.astype(BF16)
    low = (x - high.astype(F32)).astype(BF16)
    ref[pl.ds(row, 16), at] = high
    ref[pl.ds(depth + row, 16), at] = low


def repeat(count, step):
    for n in range(count):
        step(n, 0)


def main_kernel(
    recv_ref,
    outer_ref,
    inner_ref,
    cell_ref,
    live_ref,
    own_ref,
    shift_ref,
    win_ref,
    w3_ref,
    wlat_ref,
    wlat_t_ref,
    w3_t_ref,
    win_t_ref,
    read_ref,
    msg_ref,
    ext_ref,
    local_ref,
    hot,
    harm,
    env_live,
    pre,
    slope,
    cat_a,
    cat_b,
    mixed,
    paths,
    environment,
    grad_lat,
    grad_harm,
    grad_env,
    energy,
):
    blocks = [slice(b * LANES, (b + 1) * LANES) for b in range(BLOCKS)]

    columns = from_rows([recv_ref[pl.ds(neighbour(n), 1), :] for n in range(8)])
    columns += [pad_rows(outer_ref[...]), pad_rows(inner_ref[...])]
    extended = jnp.concatenate(columns, axis=1) + shift_ref[...]
    cells = lax.broadcasted_iota(jnp.int32, (512, EDGES), 0)
    hot[...] = jnp.where(cells == cell_ref[...], 1.0, 0.0).astype(BF16)
    partner = exact_dot(extended, hot[...])
    own = own_ref[...]
    center = jnp.concatenate([own[:, :LANES]] * 8 + [own[:, LANES:]], axis=1)
    displacement = partner - center

    def wide(x, row):
        return jnp.broadcast_to(x[row : row + 1], (8, EDGES))

    x = wide(displacement, 0) * 0.2
    y = wide(displacement, 1) * 0.2
    z = wide(displacement, 2) * 0.2
    scaled = x * x + y * y + z * z
    live = jnp.broadcast_to(live_ref[...], (8, EDGES))
    env_live[...] = (1.0 - scaled) * (1.0 - scaled) * live
    harm[0] = x
    harm[1] = y
    harm[2] = z
    harm[3] = ROOT3 * x * y
    harm[4] = ROOT3 * y * z
    harm[5] = ROOT3 * x * z
    harm[6] = (0.5 * ROOT3) * (x * x - y * y)
    harm[7] = 0.5 * (2.0 * z * z - x * x - y * y)

    order = lax.broadcasted_iota(jnp.int32, (8, EDGES), 0)
    orders = order.astype(F32)
    radial, radial_sin = cos_sin_pi(orders * scaled)
    kinds = jnp.where(order < 4, wide(center, 3), wide(partner, 3) + 4.0)
    one_hot = jnp.where(kinds == orders, 1.0, 0.0)
    inputs = jnp.concatenate([radial, one_hot], axis=0)
    inputs_high = inputs.astype(BF16)
    inputs_low = (inputs - inputs_high.astype(F32)).astype(BF16)
    pre[...] = dot_cat(win_ref[...], jnp.concatenate([inputs_high, inputs_low], axis=0)).reshape(16, 8, EDGES)

    def first_layer(c, carry):
        v = pre[pl.ds(2 * c, 2)]
        gate = 1.0 / (1.0 + jnp.exp(-v))
        out = v * gate
        slope[pl.ds(2 * c, 2)] = gate + out * (1.0 - gate)
        store_cat(cat_a, 16 * c, 128, slice(None), out.reshape(16, EDGES))
        return carry

    repeat(8, first_layer)
    mixed[...] = dot_cat(w3_ref[...], cat_a[...]).reshape(24, 8, EDGES)

    def forward_tile(t, carry):
        sums = [[None, None] for _ in range(9)]
        for b, at in enumerate(blocks):
            weight = mixed[pl.ds(8 + 2 * t, 2), :, at] * env_live[:, at]
            part = 0 if b < 8 else 1
            for r in range(9):
                term = weight if r == 0 else weight * harm[r - 1, :, at]
                sums[r][part] = term if sums[r][part] is None else sums[r][part] + term
        found = []
        for r in range(9):
            main, last = sum_slots(sums[r][0].reshape(16, LANES), sums[r][1].reshape(16, LANES))
            main, last = main.reshape(2, 8, LANES), last.reshape(2, 8, LANES)
            environment[r, pl.ds(2 * t, 2), :, 0:LANES] = main
            environment[r, pl.ds(2 * t, 2), :, LANES : 2 * LANES] = last
            found.append((main, last))
        for b, at in enumerate(blocks):
            part = 0 if b < 8 else 1
            h = [None] + [harm[r, :, at] for r in range(8)]
            e = [found[r][part] for r in range(9)]
            one = h[1] * e[1] + h[2] * e[2] + h[3] * e[3]
            two = h[4] * e[4] + h[5] * e[5] + h[6] * e[6] + h[7] * e[7] + h[8] * e[8]
            paths[0, pl.ds(2 * t, 2), :, at] = one
            paths[1, pl.ds(2 * t, 2), :, at] = two
            values = mixed[pl.ds(16 + 2 * t, 2), :, at]
            base = 16 * t
            store_cat(cat_b, base, 256, at, mixed[pl.ds(2 * t, 2), :, at].reshape(16, LANES))
            store_cat(cat_b, 64 + base, 256, at, (e[0] * values).reshape(16, LANES))
            store_cat(cat_b, 128 + base, 256, at, (one * values).reshape(16, LANES))
            store_cat(cat_b, 192 + base, 256, at, (two * values).reshape(16, LANES))
        return carry

    repeat(4, forward_tile)
    pre[...] = dot_cat(wlat_ref[...], cat_b[...]).reshape(16, 8, EDGES)
    energy[...] = jnp.zeros((8, EDGES), F32)

    def second_layer(c, carry):
        v = pre[pl.ds(2 * c, 2)]
        gate = 1.0 / (1.0 + jnp.exp(-v))
        out = v * gate
        weights = read_ref[pl.ds(16 * c, 16), :].reshape(2, 8, LANES)
        weights = jnp.concatenate([weights] * BLOCKS, axis=2)
        product = weights * out
        energy[...] += product[0] + product[1]
        back = weights * (gate + out * (1.0 - gate)) * env_live[...]
        store_cat(cat_a, 16 * c, 128, slice(None), back.reshape(16, EDGES))
        return carry

    repeat(8, second_layer)
    grad_lat[...] = dot_cat(wlat_t_ref[...], cat_a[...]).reshape(32, 8, EDGES)
    grad_harm[...] = jnp.zeros((8, 8, EDGES), F32)
    grad_env[...] = jnp.zeros((8, EDGES), F32)

    def backward_tile(t, carry):
        base = 16 * t
        sums = [[None, None] for _ in range(9)]
        for b, at in enumerate(blocks):
            part = 0 if b < 8 else 1
            lanes = slice(part * LANES, (part + 1) * LANES)
            values = mixed[pl.ds(16 + 2 * t, 2), :, at]
            d = [grad_lat[pl.ds(8 + 8 * l + 2 * t, 2), :, at] for l in range(3)]
            zero = environment[0, pl.ds(2 * t, 2), :, lanes]
            one = paths[0, pl.ds(2 * t, 2), :, at]
            two = paths[1, pl.ds(2 * t, 2), :, at]
            d_values = d[0] * zero + d[1] * one + d[2] * two
            store_cat(cat_b, 128 + base, 192, at, d_values.reshape(16, LANES))
            store_cat(cat_b, base, 192, at, grad_lat[pl.ds(2 * t, 2), :, at].reshape(16, LANES))
            q = [d[l] * values for l in range(3)]
            for r in range(9):
                level = 0 if r == 0 else (1 if r < 4 else 2)
                term = q[0] if r == 0 else q[level] * harm[r - 1, :, at]
                sums[r][part] = term if sums[r][part] is None else sums[r][part] + term
        found = []
        for r in range(9):
            main, last = sum_slots(sums[r][0].reshape(16, LANES), sums[r][1].reshape(16, LANES))
            found.append((main.reshape(2, 8, LANES), last.reshape(2, 8, LANES)))
        for b, at in enumerate(blocks):
            part = 0 if b < 8 else 1
            lanes = slice(part * LANES, (part + 1) * LANES)
            raw = mixed[pl.ds(8 + 2 * t, 2), :, at]
            envelope = env_live[:, at]
            weight = raw * envelope
            values = mixed[pl.ds(16 + 2 * t, 2), :, at]
            q = [None] + [grad_lat[pl.ds(8 + 8 * l + 2 * t, 2), :, at] * values for l in (1, 2)]
            d_weight = found[0][part]
            for r in range(1, 9):
                g = found[r][part]
                d_weight = d_weight + harm[r - 1, :, at] * g
                level = 1 if r < 4 else 2
                term = q[level] * environment[r, pl.ds(2 * t, 2), :, lanes] + weight * g
                grad_harm[r - 1, :, at] += term[0] + term[1]
            slack = d_weight * raw
            grad_env[:, at] += slack[0] + slack[1]
            store_cat(cat_b, 64 + base, 192, at, (d_weight * envelope).reshape(16, LANES))
        return carry

    repeat(4, backward_tile)
    pre[...] = dot_cat(w3_t_ref[...], cat_b[0:384]).reshape(16, 8, EDGES)

    def first_back(c, carry):
        back = pre[pl.ds(2 * c, 2)] * slope[pl.ds(2 * c, 2)]
        store_cat(cat_a, 16 * c, 128, slice(None), back.reshape(16, EDGES))
        return carry

    repeat(8, first_back)
    d_radial = dot_cat(win_t_ref[...], cat_a[...])[:8]

    x, y, z = harm[0], harm[1], harm[2]
    scaled = x * x + y * y + z * z
    live = jnp.broadcast_to(live_ref[...], (8, EDGES))
    d_scaled = d_radial * (orders * radial_sin) * (-math.pi) + (grad_env[...] + energy[...]) * (
        -2.0 * (1.0 - scaled) * live
    )
    g = [grad_harm[r] for r in range(8)]
    twice = 2.0 * d_scaled
    d_x = g[0] + ROOT3 * (y * g[3] + z * g[5] + x * g[6]) - x * g[7] + twice * x
    d_y = g[1] + ROOT3 * (x * g[3] + z * g[4] - y * g[6]) - y * g[7] + twice * y
    d_z = g[2] + ROOT3 * (y * g[4] + x * g[5]) + 2.0 * z * g[7] + twice * z
    e = energy[...] * env_live[...]
    partial = [d_x * 0.2, d_y * 0.2, d_z * 0.2]
    extended_grad = exact_dot_nt(jnp.concatenate(partial, axis=0), hot[...], 2)

    def over_blocks(v):
        total = v[:, blocks[0]]
        for b in range(1, 8):
            total = total + v[:, blocks[b]]
        return total

    def summed(arrays):
        rows = [jnp.sum(v, axis=0, keepdims=True) for v in arrays]
        return jnp.concatenate(rows + [jnp.zeros((8 - len(rows), rows[0].shape[1]), F32)], axis=0)

    virial = []
    for a, comp in enumerate((x, y, z)):
        for b in range(3):
            product = comp * partial[b]
            virial.append(over_blocks(product) + product[:, blocks[8]])
    totals = jnp.sum(jnp.concatenate(virial, axis=0), axis=1, keepdims=True)
    lane = lax.broadcasted_iota(jnp.int32, (8, LANES), 1)
    virial = jnp.zeros((8, LANES), F32)
    for n in range(9):
        virial = jnp.where(lane == 96 + n, totals[8 * n : 8 * n + 8] * 5.0, virial)
    virial = jnp.sum(virial, axis=0, keepdims=True)

    extended_grad = summed([extended_grad[8 * c : 8 * c + 8] for c in range(3)])
    rows = to_rows(extended_grad[:, :256])
    msg_ref[...] = jnp.broadcast_to(virial, (COUNT * COUNT, LANES))
    for n in range(8):
        msg_ref[pl.ds(neighbour(n), 1), :] = rows[n] + virial
    ext_ref[...] = extended_grad[:4, 256:]

    arrays = partial + [e]
    main, last = sum_slots(summed([over_blocks(v) for v in arrays]), summed([v[:, blocks[8]] for v in arrays]))
    local_ref[...] = jnp.concatenate([main[:, :MAIN], last[:, : ATOMS - MAIN]], axis=1)


def middle_kernel(recv_ref, ext_ref, routes_ref, msg_ref, keep_ref):
    columns = from_rows([recv_ref[pl.ds(neighbour(n), 1), :] for n in range(8)])
    sums = exact_dot_nt(jnp.concatenate(columns, axis=1), routes_ref[...], 2) + pad_rows(ext_ref[...])
    total = jnp.sum(recv_ref[...], axis=0, keepdims=True)
    message = jnp.concatenate([sums[:3, :LANES], total], axis=0)
    msg_ref[...] = jnp.broadcast_to(message[None], (COUNT, 4, LANES))
    keep_ref[...] = sums[:, LANES:]


def last_kernel(recv_ref, keep_ref, local_ref, hot_ref, force_ref, energy_ref, virial_ref):
    gz = lax.axis_index("gz")
    above = pad_rows(recv_ref[lax.rem(gz + 1, COUNT)])
    below = pad_rows(recv_ref[lax.rem(gz + (COUNT - 1), COUNT)])
    lane = lax.broadcasted_iota(jnp.int32, (8, LANES), 1)
    row = lax.broadcasted_iota(jnp.int32, (8, LANES), 0)
    sites = keep_ref[...] + jnp.where(lane < 64, pltpu.roll(below, 64, 1), pltpu.roll(above, 64, 1))
    atoms = exact_dot_nt(sites, hot_ref[...], 2)
    energy_ref[...] = local_ref[3:4]
    force = local_ref[...] - atoms
    for comp in range(3):
        force_ref[comp] = force[comp : comp + 1]
    total = jnp.broadcast_to(jnp.sum(recv_ref[...], axis=0)[3:4], (8, LANES))
    normalizer = -1.0 / math.sqrt(EDGES * COUNT * COUNT * COUNT)
    virial = jnp.zeros((8, LANES), F32)
    for b in range(3):
        entry = jnp.sum(jnp.where(lane == 96 + 3 * row + b, total, 0.0), axis=1, keepdims=True)
        virial = jnp.where(lane == b, entry * normalizer, virial)
    virial_ref[...] = virial[:3, :3]


def shape(*dims, dtype=F32):
    return jax.ShapeDtypeStruct(dims, dtype)


def in_hbm(*arrays):
    return [pltpu.with_memory_space_constraint(x, pltpu.HBM) for x in arrays]


def params():
    return pltpu.CompilerParams(vmem_limit_bytes=48 * 1024 * 1024)


def body(
    positions,
    species,
    site_atom,
    edge_center,
    edge_other,
    edge_count,
    w_in,
    w_two,
    w_env,
    w_value,
    w_latent,
    w_out,
    readout,
):
    half = (4, LANES)
    hbm = pl.BlockSpec(memory_space=pltpu.HBM)
    inputs = (
        site_atom,
        jnp.transpose(positions, (1, 0, 2)),
        species,
        edge_center,
        edge_other,
        w_out,
        readout.reshape(1, 64),
        w_two,
        w_env,
        w_value,
        w_latent,
        w_in.T,
    )
    own, first, second, hot, *copied = pl.pallas_call(
        send_kernel,
        in_specs=[hbm] * len(inputs),
        out_shape=(shape(*half), shape(2, LANES), shape(2, LANES), shape(ATOMS, LANES, dtype=BF16))
        + tuple(shape(*x.shape, dtype=x.dtype) for x in inputs[1:]),
        scratch_shapes=[pltpu.VMEM((1, ATOMS), jnp.int32), pltpu.SemaphoreType.DMA((len(inputs),))],
        compiler_params=params(),
        name="sites",
    )(*in_hbm(*inputs))
    first = lax.ppermute(first, "gz", [(i, ((i - 1) ^ 1) + 1 & 7) for i in range(COUNT)])
    second = lax.ppermute(second, "gz", [(i, i ^ 1) for i in range(COUNT)])

    vmem = pl.BlockSpec(memory_space=pltpu.VMEM)
    *prepared, routes = pl.pallas_call(
        prepare_kernel,
        in_specs=[pl.BlockSpec(memory_space=pltpu.SMEM)] + [vmem] * len(copied) + [hbm],
        out_shape=(
            shape(1, EDGES, dtype=jnp.int32),
            shape(1, EDGES),
            shape(8, 256),
            shape(8, 512),
            shape(256, 32, dtype=BF16),
            shape(384, 256, dtype=BF16),
            shape(256, 512, dtype=BF16),
            shape(512, 256, dtype=BF16),
            shape(256, 384, dtype=BF16),
            shape(32, 256, dtype=BF16),
            shape(128, LANES),
            shape(256, 256, dtype=BF16),
        ),
        scratch_shapes=[pltpu.SemaphoreType.DMA(())],
        compiler_params=params(),
        cost_estimate=pl.CostEstimate(flops=10_000_000, bytes_accessed=2_000_000, transcendentals=0),
        name="slots_and_weights",
    )(edge_count, *copied, *in_hbm(jnp.asarray(ROUTES, BF16)))

    planes = (COUNT * COUNT, LANES)
    column, outer = pl.pallas_call(
        column_kernel,
        out_shape=(shape(*planes), shape(*half)),
        compiler_params=params(),
        name="column",
    )(own, first, second, routes)
    arrived = lax.all_to_all(column, ("gx", "gy"), 0, 0)

    message, extended_grad, local_grad = pl.pallas_call(
        main_kernel,
        out_shape=(shape(*planes), shape(4, 256), shape(8, ATOMS)),
        scratch_shapes=[
            pltpu.VMEM((512, EDGES), BF16),
            pltpu.VMEM((8, 8, EDGES), F32),
            pltpu.VMEM((8, EDGES), F32),
            pltpu.VMEM((16, 8, EDGES), F32),
            pltpu.VMEM((16, 8, EDGES), F32),
            pltpu.VMEM((256, EDGES), BF16),
            pltpu.VMEM((512, EDGES), BF16),
            pltpu.VMEM((24, 8, EDGES), F32),
            pltpu.VMEM((2, 8, 8, EDGES), F32),
            pltpu.VMEM((9, 8, 8, 256), F32),
            pltpu.VMEM((32, 8, EDGES), F32),
            pltpu.VMEM((8, 8, EDGES), F32),
            pltpu.VMEM((8, EDGES), F32),
            pltpu.VMEM((8, EDGES), F32),
        ],
        compiler_params=params(),
        name="edges",
    )(arrived, outer, own, *prepared)
    returned = lax.all_to_all(message, ("gx", "gy"), 0, 0)
    layers, keep = pl.pallas_call(
        middle_kernel,
        out_shape=(shape(COUNT, 4, LANES), shape(8, LANES)),
        compiler_params=params(),
        name="columns_back",
    )(returned, extended_grad, routes)
    closing = lax.all_to_all(layers, "gz", 0, 0)
    forces, site_energy, virial = pl.pallas_call(
        last_kernel,
        out_shape=(shape(3, 1, ATOMS), shape(1, ATOMS), shape(3, 3)),
        compiler_params=params(),
        name="forces",
    )(closing, keep, local_grad, hot)
    return jnp.transpose(forces, (1, 0, 2)), site_energy, virial


def solution(mesh):
    by_domain = ("gx", "gy", "gz")
    placed = (
        P(by_domain, None, None),
        P(by_domain, None),
        P(by_domain, None),
        P(by_domain, None),
        P(by_domain, None),
        P(by_domain),
    ) + (P(),) * 7
    return jax.shard_map(
        body,
        mesh=mesh,
        in_specs=placed,
        out_specs=(P(by_domain, None, None), P(by_domain, None), P()),
        check_vma=False,
    )
```
